512 devices in a mesh: seq: 128 (over z, x, y_lo), head: 4 (over y_hi, core).
Axes of the slice: x: 4, y: 8 (y_hi: 2, y_lo: 4; y = y_hi * 4 + y_lo), z: 8, core: 2. Of those that a mesh axis runs over, the one named last changes fastest.
Arguments:
- query_rows: bfloat16 [32768, 1536], P('seq', 'head'), may hold values from -6 to 6
- key_rows: bfloat16 [32768, 1536], P('seq', 'head'), may hold values from -6 to 6
- value_rows: bfloat16 [32768, 1536], P('seq', 'head'), may hold values from -4 to 4
- out_weight: bfloat16 [1536, 1536], P(None, 'head'), may hold values from -0.15625 to 0.15625
- out_grad: bfloat16 [32768, 1536], P('seq', 'head'), may hold values from -24 to 24
Outputs:
- projected: bfloat16 [32768, 1536], P('seq', 'head')
- query_grad: bfloat16 [32768, 1536], P('seq', 'head')
- key_grad: bfloat16 [32768, 1536], P('seq', 'head')
- value_grad: bfloat16 [32768, 1536], P('seq', 'head')
- weight_grad: float32 [1536, 1536], P('seq', 'head')
The draws below stay inside these ranges and needn't reach their ends.
All inputs are finite; a program needn't handle non-finite values.
Results may differ from the reference program's by a relative error of at most 0.035.
Values may be sent and summed in bfloat16 or wider, within the bound.
A program may use at most 64 MiB of HBM per device.

```python
import jax
import jax.numpy as jnp
from jax import lax

D = 1536
HEADS = 24
HEAD_DIM = 64
SPAN = 256
LOOKBACK = 4
FRAMES = 32768
N_SEQ = 128


def draw_query_rows(key, part):
    key = jax.random.fold_in(key, 11)
    values = jnp.clip(jax.random.normal(key, (FRAMES, D), jnp.float32), -4.0, 4.0)
    return values.astype(jnp.bfloat16)


def draw_key_rows(key, part):
    key = jax.random.fold_in(key, 23)
    values = jnp.clip(jax.random.normal(key, (FRAMES, D), jnp.float32), -4.0, 4.0)
    return values.astype(jnp.bfloat16)


def with_spikes(array, rng, source, target, shards_of, factor):
    def block_of(axis_at):
        return (jnp.arange(array.shape[axis_at]) // (array.shape[axis_at] // shards_of)).reshape((-1,) + (1,) * (array.ndim - 1 - axis_at))

    near = jax.random.permutation(rng, shards_of)[block_of(target)]
    far = (block_of(target) + shards_of // 2) % shards_of
    return jnp.where((block_of(source) == near) | (block_of(source) == far), factor * array, array)


def shard_levels(own_key, dims, shards, low, high):
    factor_of = 1.0
    for dim, parts in shards:
        draws = jax.random.uniform(jax.random.fold_in(jax.random.fold_in(own_key, 6), dim), (parts,), jnp.float32, low / len(shards), high / len(shards))
        factor_of = factor_of * jnp.repeat(jnp.exp(draws), dims[dim] // parts).reshape((-1,) + (1,) * (len(dims) - 1 - dim))
    return factor_of


def centred(key, dims, spread, reach, cuts=(), kind=jnp.bfloat16):
    result = jax.random.normal(key, dims, jnp.float32) * spread
    if len(cuts) > 0:
        result = shard_levels(key, dims, cuts, -0.22, 0.18) * result
    return jnp.clip(result, min=-reach, max=reach).astype(kind)


def gaussian_with(stream_key, shape, width, limit, shards, heavy, held_as=jnp.bfloat16):
    entries = width * jax.random.normal(stream_key, shape, jnp.float32)
    if shards:
        entries = entries * shard_levels(stream_key, shape, shards, -0.22, 0.18)
    return jnp.clip(with_spikes(entries, jax.random.fold_in(stream_key, 3), *heavy), -limit, limit).astype(held_as)


def setup_inputs(seed: int = 0) -> dict:
    seeds = jax.random.split(jax.random.key(seed), 6)
    return {
        "query_rows": draw_query_rows(jax.random.fold_in(seeds[5], 71), 0),
        "key_rows": draw_key_rows(jax.random.fold_in(seeds[5], 71), 0),
        "value_rows": centred(seeds[2], (FRAMES, D), 1.0, 4.0, ((0, 128), (1, 4))),
        "out_weight": centred(seeds[3], (D, D), D ** -0.5, 0.15625, ((1, 4),)),
        "out_grad": gaussian_with(seeds[4], (FRAMES, D), 1.0, 24.0, ((0, 128), (1, 4)), (0, 1, 128, 5.5)),
    }


def window_probs(query_blk, key_blk, key_valid, score_scale):
    scores = jnp.einsum('qhe,khe->hqk', query_blk.astype(jnp.float32), key_blk.astype(jnp.float32)) * score_scale
    scores = jnp.where(key_valid[None, None, :], scores, -jnp.inf)
    row_max = jnp.max(scores, axis=-1, keepdims=True)
    exp_scores = jnp.exp(scores - row_max)
    return exp_scores / jnp.sum(exp_scores, axis=-1, keepdims=True)


def reference(query_rows, key_rows, value_rows, out_weight, out_grad):
    score_scale = float(HEAD_DIM) ** -0.5
    window = (LOOKBACK + 1) * SPAN
    padding = jnp.zeros((LOOKBACK * SPAN, D), jnp.bfloat16)
    key_padded = jnp.concatenate([padding, key_rows], axis=0)
    value_padded = jnp.concatenate([padding, value_rows], axis=0)
    block_of = jnp.arange(window, dtype=jnp.int32) // SPAN

    def per_span(carry, span_idx):
        key_acc, value_acc = carry
        row_start = (span_idx * SPAN).astype(jnp.int32)
        query_blk = lax.dynamic_slice_in_dim(query_rows, row_start, SPAN, 0).reshape(SPAN, HEADS, HEAD_DIM)
        key_blk = lax.dynamic_slice_in_dim(key_padded, row_start, window, 0).reshape(window, HEADS, HEAD_DIM)
        value_blk = lax.dynamic_slice_in_dim(value_padded, row_start, window, 0).reshape(window, HEADS, HEAD_DIM)
        key_valid = span_idx - LOOKBACK + block_of >= 0
        attn_probs = window_probs(query_blk, key_blk, key_valid, score_scale)
        probs_low = attn_probs.astype(jnp.bfloat16)
        attended = jnp.einsum('hqk,khe->qhe', probs_low.astype(jnp.float32), value_blk.astype(jnp.float32)).astype(jnp.bfloat16)
        grad_blk = lax.dynamic_slice_in_dim(out_grad, row_start, SPAN, 0)
        d_attended = jnp.dot(grad_blk, out_weight, preferred_element_type=jnp.float32).astype(jnp.bfloat16)
        d_attended = d_attended.reshape(SPAN, HEADS, HEAD_DIM)
        row_delta = jnp.einsum('qhe,qhe->hq', d_attended.astype(jnp.float32), attended.astype(jnp.float32))
        d_probs = jnp.einsum('qhe,khe->hqk', d_attended.astype(jnp.float32), value_blk.astype(jnp.float32))
        d_scores = (attn_probs * (d_probs - row_delta[:, :, None])).astype(jnp.bfloat16)
        query_part = jnp.einsum('hqk,khe->qhe', d_scores.astype(jnp.float32), key_blk.astype(jnp.float32)) * score_scale
        key_part = jnp.einsum('hqk,qhe->khe', d_scores.astype(jnp.float32), query_blk.astype(jnp.float32)) * score_scale
        value_part = jnp.einsum('hqk,qhe->khe', probs_low.astype(jnp.float32), d_attended.astype(jnp.float32))
        old_keys = lax.dynamic_slice_in_dim(key_acc, row_start, window, 0)
        key_acc = lax.dynamic_update_slice_in_dim(key_acc, old_keys + key_part.reshape(window, D), row_start, 0)
        old_values = lax.dynamic_slice_in_dim(value_acc, row_start, window, 0)
        value_acc = lax.dynamic_update_slice_in_dim(value_acc, old_values + value_part.reshape(window, D), row_start, 0)
        return (key_acc, value_acc), (attended.reshape(SPAN, D), query_part.reshape(SPAN, D).astype(jnp.bfloat16))

    zeros_acc = jnp.zeros(((N_SEQ + LOOKBACK) * SPAN, D), jnp.float32)
    (key_acc, value_acc), (attended, query_grad) = lax.scan(
        per_span, (zeros_acc, zeros_acc), jnp.arange(N_SEQ, dtype=jnp.int32))
    attended = attended.reshape(FRAMES, D)
    query_grad = query_grad.reshape(FRAMES, D)
    projected = jnp.dot(attended, out_weight.T, preferred_element_type=jnp.float32).astype(jnp.bfloat16)
    key_grad = key_acc[LOOKBACK * SPAN:].astype(jnp.bfloat16)
    value_grad = value_acc[LOOKBACK * SPAN:].astype(jnp.bfloat16)
    weight_grad = jnp.dot(out_grad.T, attended, preferred_element_type=jnp.float32)
    return (projected, query_grad, key_grad, value_grad, weight_grad)
```

```python
import functools

import jax
import jax.numpy as jnp
from jax import lax
from jax.experimental import pallas as pl
from jax.experimental.pallas import tpu as pltpu
from jax.sharding import PartitionSpec as P

MESH = pl.DeviceIdType.MESH
D = 1536
HEADS = 24
LOOKBACK = 4


def shifted(block, axis, distance):
    devices = range(lax.axis_size(axis))
    route = [(i - distance, i) for i in devices if i - distance in devices]
    return lax.ppermute(block, axis, route)


def window_probs(query_grp, key_grp, key_valid, score_scale):
    scores = (
        jnp.einsum("qhe,khe->hqk", query_grp, key_grp, preferred_element_type=jnp.float32)
        * score_scale
    )
    scores = jnp.where(key_valid[None, None, :], scores, -jnp.inf)
    row_max = jnp.max(scores, axis=-1, keepdims=True)
    exp_scores = jnp.exp(scores - row_max)
    return exp_scores / jnp.sum(exp_scores, axis=-1, keepdims=True)


X_SIZE = 4
Y_SIZE = 4


def weight_sum_kernel(z_size, terms_ref, out_ref, x_in, z_send, z_in, y_send, y_in, sums, x_sems, z_sems, y_sems):
    seq = lax.axis_index("seq")
    head = lax.axis_index("head")
    y_at = seq % Y_SIZE
    x_at = (seq // Y_SIZE) % X_SIZE
    z_at = seq // (Y_SIZE * X_SIZE)

    def device(z, x, y):
        return ((z * X_SIZE + x) * Y_SIZE + y, head)

    def x_peer(step):
        return (x_at + step) % X_SIZE

    def z_peer(step):
        return (z_at + step) % z_size

    def y_peer(step):
        return (y_at + step) % Y_SIZE

    barrier = pltpu.get_barrier_semaphore()
    for step in range(1, X_SIZE):
        pl.semaphore_signal(barrier, inc=1, device_id=device(z_at, x_peer(step), y_at), device_id_type=MESH)
    for step in range(1, z_size):
        pl.semaphore_signal(barrier, inc=1, device_id=device(z_peer(step), x_at, y_at), device_id_type=MESH)
    for step in range(1, Y_SIZE):
        pl.semaphore_signal(barrier, inc=1, device_id=device(z_at, x_at, y_peer(step)), device_id_type=MESH)
    pl.semaphore_wait(barrier, X_SIZE + Y_SIZE + z_size - 3)

    x_copies = []
    for step in range(1, X_SIZE):
        copy = pltpu.make_async_remote_copy(
            src_ref=terms_ref.at[:, x_peer(step)],
            dst_ref=x_in.at[step - 1],
            send_sem=x_sems.at[0, step - 1],
            recv_sem=x_sems.at[1, step - 1],
            device_id=device(z_at, x_peer(step), y_at),
            device_id_type=MESH,
        )
        copy.start()
        x_copies.append(copy)
    for copy in x_copies:
        copy.wait_recv()
    total = terms_ref[:, x_at].astype(jnp.float32)
    for step in range(1, X_SIZE):
        total += x_in[step - 1].astype(jnp.float32)
    z_send[...] = total.astype(jnp.bfloat16)
    z_copies = []
    for step in range(1, z_size):
        copy = pltpu.make_async_remote_copy(
            src_ref=z_send.at[z_peer(step)],
            dst_ref=z_in.at[step - 1],
            send_sem=z_sems.at[0, step - 1],
            recv_sem=z_sems.at[1, step - 1],
            device_id=device(z_peer(step), x_at, y_at),
            device_id_type=MESH,
        )
        copy.start()
        z_copies.append(copy)
    for copy in z_copies:
        copy.wait_recv()
    sums[...] = z_send[z_at].astype(jnp.float32)
    for step in range(1, z_size):
        sums[...] += z_in[step - 1].astype(jnp.float32)
    rows = out_ref.shape[0]
    for piece in range(Y_SIZE):
        y_send[piece, 0:rows] = sums[piece * rows : (piece + 1) * rows]
    y_copies = []
    for step in range(1, Y_SIZE):
        copy = pltpu.make_async_remote_copy(
            src_ref=y_send.at[y_peer(step)],
            dst_ref=y_in.at[step - 1],
            send_sem=y_sems.at[0, step - 1],
            recv_sem=y_sems.at[1, step - 1],
            device_id=device(z_at, x_at, y_peer(step)),
            device_id_type=MESH,
        )
        copy.start()
        y_copies.append(copy)
    result = y_send[y_at]
    for step in range(1, Y_SIZE):
        y_copies[step - 1].wait_recv()
        result += y_in[step - 1]
    out_ref[...] = result[0:rows]
    for copy in x_copies + z_copies + y_copies:
        copy.wait_send()


def weight_sum(terms):
    seq_size = lax.axis_size("seq")
    z_size = seq_size // (X_SIZE * Y_SIZE)
    width = terms.shape[1]
    rows = terms.shape[0] // seq_size
    block = rows * Y_SIZE
    padded = (rows + 7) // 8 * 8
    return pl.pallas_call(
        functools.partial(weight_sum_kernel, z_size),
        out_shape=jax.ShapeDtypeStruct((rows, width), jnp.float32),
        in_specs=[pl.BlockSpec(memory_space=pltpu.VMEM)],
        out_specs=pl.BlockSpec(memory_space=pltpu.VMEM),
        scratch_shapes=[
            pltpu.VMEM((X_SIZE - 1, z_size, block, width), jnp.bfloat16),
            pltpu.VMEM((z_size, block, width), jnp.bfloat16),
            pltpu.VMEM((z_size - 1, block, width), jnp.bfloat16),
            pltpu.VMEM((Y_SIZE, padded, width), jnp.float32),
            pltpu.VMEM((Y_SIZE - 1, padded, width), jnp.float32),
            pltpu.VMEM((block, width), jnp.float32),
            pltpu.SemaphoreType.DMA((2, X_SIZE - 1)),
            pltpu.SemaphoreType.DMA((2, z_size - 1)),
            pltpu.SemaphoreType.DMA((2, Y_SIZE - 1)),
        ],
        compiler_params=pltpu.CompilerParams(
            collective_id=0, has_side_effects=True, vmem_limit_bytes=32 * 1024 * 1024
        ),
    )(terms.reshape(z_size, X_SIZE, block, width))


def shards(query_rows, key_rows, value_rows, out_weight, out_grad):
    span_len = query_rows.shape[0]
    width_local = query_rows.shape[1]
    heads_local = HEADS // lax.axis_size("head")
    head_width = width_local // heads_local
    score_scale = float(head_width) ** (-0.5)
    window = (LOOKBACK + 1) * span_len
    position = lax.axis_index("seq")
    earlier = []
    for offset in range(LOOKBACK, 0, -1):
        earlier.append(shifted((key_rows, value_rows), "seq", offset))
    key_window = jnp.concatenate([member[0] for member in earlier] + [key_rows], axis=0)
    value_window = jnp.concatenate([member[1] for member in earlier] + [value_rows], axis=0)
    block_of = jnp.arange(window, dtype=jnp.int32) // span_len
    key_valid = position - LOOKBACK + block_of >= 0
    per_group = 2
    groups = heads_local // per_group
    group_cols = per_group * head_width

    def group_inputs(group_idx):
        first_col = group_idx * group_cols
        query_grp = query_rows[:, first_col : first_col + group_cols].reshape(
            span_len, per_group, head_width
        )
        key_grp = key_window[:, first_col : first_col + group_cols].reshape(
            window, per_group, head_width
        )
        value_grp = value_window[:, first_col : first_col + group_cols].reshape(
            window, per_group, head_width
        )
        return (query_grp, key_grp, value_grp)

    pieces = []
    kept_probs = []
    for group_idx in range(groups):
        query_grp, key_grp, value_grp = group_inputs(group_idx)
        attn_probs = window_probs(query_grp, key_grp, key_valid, score_scale)
        kept_probs.append(attn_probs)
        probs_low = attn_probs.astype(jnp.bfloat16)
        pieces.append(
            jnp.einsum(
                "hqk,khe->qhe", probs_low, value_grp, preferred_element_type=jnp.float32
            ).reshape(span_len, group_cols)
        )
    attended = jnp.concatenate(pieces, axis=1).astype(jnp.bfloat16)
    partial_value = lax.dot_general(
        attended, out_weight, (((1,), (1,)), ((), ())), preferred_element_type=jnp.float32
    )
    summed_all = lax.psum(partial_value, "head")
    out_width = D // lax.axis_size("head")
    projected = lax.dynamic_slice_in_dim(
        summed_all, lax.axis_index("head") * out_width, out_width, 1
    )
    projected = projected.astype(jnp.bfloat16)
    grad_full = lax.all_gather(out_grad, "head", axis=1, tiled=True)
    d_attended = jnp.dot(grad_full, out_weight, preferred_element_type=jnp.float32).astype(
        jnp.bfloat16
    )
    query_pieces = []
    key_pieces = []
    value_pieces = []
    for group_idx in range(groups):
        query_grp, key_grp, value_grp = group_inputs(group_idx)
        first_col = group_idx * group_cols
        dout_grp = d_attended[:, first_col : first_col + group_cols].reshape(
            span_len, per_group, head_width
        )
        attn_grp = attended[:, first_col : first_col + group_cols].reshape(
            span_len, per_group, head_width
        )
        attn_probs = kept_probs[group_idx]
        probs_low = attn_probs.astype(jnp.bfloat16)
        row_delta = jnp.einsum(
            "qhe,qhe->hq", dout_grp.astype(jnp.float32), attn_grp.astype(jnp.float32)
        )
        d_probs = jnp.einsum(
            "qhe,khe->hqk", dout_grp, value_grp, preferred_element_type=jnp.float32
        )
        d_scores = (attn_probs * (d_probs - row_delta[:, :, None])).astype(jnp.bfloat16)
        query_pieces.append(
            (
                jnp.einsum("hqk,khe->qhe", d_scores, key_grp, preferred_element_type=jnp.float32)
                * score_scale
            ).reshape(span_len, group_cols)
        )
        key_pieces.append(
            (
                jnp.einsum("hqk,qhe->khe", d_scores, query_grp, preferred_element_type=jnp.float32)
                * score_scale
            ).reshape(window, group_cols)
        )
        value_pieces.append(
            jnp.einsum(
                "hqk,qhe->khe", probs_low, dout_grp, preferred_element_type=jnp.float32
            ).reshape(window, group_cols)
        )
    query_grad = jnp.concatenate(query_pieces, axis=1).astype(jnp.bfloat16)
    key_terms = jnp.concatenate(key_pieces, axis=1)
    value_terms = jnp.concatenate(value_pieces, axis=1)
    own_start = LOOKBACK * span_len
    key_total = key_terms[own_start:]
    value_total = value_terms[own_start:]
    for offset in range(1, LOOKBACK + 1):
        first_row = (LOOKBACK - offset) * span_len
        arrived = shifted(
            (
                key_terms[first_row : first_row + span_len],
                value_terms[first_row : first_row + span_len],
            ),
            "seq",
            -offset,
        )
        key_total = key_total + arrived[0]
        value_total = value_total + arrived[1]
    weight_terms = lax.dot_general(
        grad_full, attended, (((0,), (0,)), ((), ())), preferred_element_type=jnp.float32
    )
    weight_grad = weight_sum(weight_terms.astype(jnp.bfloat16))
    return (
        projected,
        query_grad,
        key_total.astype(jnp.bfloat16),
        value_total.astype(jnp.bfloat16),
        weight_grad,
    )


def solution(mesh):
    in_specs = (
        P("seq", "head"),
        P("seq", "head"),
        P("seq", "head"),
        P(None, "head"),
        P("seq", "head"),
    )
    out_specs = (
        P("seq", "head"),
        P("seq", "head"),
        P("seq", "head"),
        P("seq", "head"),
        P("seq", "head"),
    )
    return jax.shard_map(shards, mesh=mesh, in_specs=in_specs, out_specs=out_specs, check_vma=False)
```

```python
import functools

import jax
import jax.numpy as jnp
from jax import lax
from jax.experimental import pallas as pl
from jax.experimental.pallas import tpu as pltpu
from jax.sharding import PartitionSpec as P

MESH = pl.DeviceIdType.MESH
BF16 = jnp.bfloat16
F32 = jnp.float32
SPAN = 256
COLS = 384
HEAD_DIM = 64
LANES = 128
HALF = 128
PIECE = SPAN + HALF
SLOTS = 6
WINDOW = 5
X_SIZE = 4
Y_SIZE = 4
HEAD_SIZE = 4
NN = (((1,), (0,)), ((), ()))
NT = (((1,), (1,)), ((), ()))
K, Q, V, DO, ATT, DQ, DK, DV = range(8)


def product(left, right, dims):
    return lax.dot_general(left, right, dims, preferred_element_type=F32)


def low_lanes(rows):
    return lax.broadcasted_iota(jnp.int32, (rows, LANES), 1) < HEAD_DIM


def swap(block):
    return pltpu.roll(block, HEAD_DIM, 1)


def fold(block):
    return jnp.where(low_lanes(HALF), block[:HALF], swap(block[HALF:]))


def to_pieces(tiles, piece_ref, scale=None):
    first, middle, last = [tile.astype(F32) for tile in tiles]
    if scale is not None:
        first, middle, last = first * scale, middle * scale, last * scale
    swapped = swap(middle)
    piece_ref[0, :SPAN] = first.astype(BF16)
    piece_ref[0, SPAN:] = jnp.where(low_lanes(HALF), middle[:HALF], swapped[HALF:]).astype(BF16)
    piece_ref[1, :SPAN] = last.astype(BF16)
    piece_ref[1, SPAN:] = jnp.where(low_lanes(HALF), swapped[:HALF], middle[HALF:]).astype(BF16)


def from_pieces(piece_ref, out_ref):
    out_ref[:, 0:LANES] = piece_ref[0, :SPAN]
    out_ref[:, 2 * LANES : 3 * LANES] = piece_ref[1, :SPAN]
    low = piece_ref[0, SPAN:].astype(F32)
    high = piece_ref[1, SPAN:].astype(F32)
    top = jnp.where(low_lanes(HALF), low, swap(high))
    bottom = jnp.where(low_lanes(HALF), swap(low), high)
    out_ref[:HALF, LANES : 2 * LANES] = top.astype(BF16)
    out_ref[HALF:, LANES : 2 * LANES] = bottom.astype(BF16)


def unfold(third):
    wide = third.astype(F32)
    return jnp.concatenate([wide, swap(wide)], axis=0)


def layer_kernel(
    z_size,
    q_ref, k_ref, v_ref, w_ref, g_ref,
    proj_ref, dq_ref, dk_ref, dv_ref, dw_ref,
    packs, q_in, do_in, k_in, v_in, att_in, dq_in, dk_in, dv_in,
    grads, grads_t, k_nat, v_nat, k_tr, v_tr, q_tr, do_tr,
    scores, weights, inverse, att_tr, dq_tr, dk_acc, dv_acc,
    back_send, back_in, attended,
    proj_send, proj_in, proj_keep, hip_send, hip_in,
    terms, x_in, z_send, z_in, y_send, y_in, sums,
    a2a_send_sems, a2a_recv_sems, flow_send_sems, flow_recv_sems, back_send_sems, back_recv_sems,
    grad_send_sems, grad_recv_sems, proj_send_sems, proj_recv_sems, x_sems, z_sems, y_sems,
):
    seq = lax.axis_index("seq")
    head = lax.axis_index("head")
    rows = z_size * X_SIZE
    y_at = seq % Y_SIZE
    row_at = seq // Y_SIZE
    x_at = row_at % X_SIZE
    z_at = row_at // X_SIZE
    core = head % 2
    high = head // 2
    y_half = y_at // 2
    y_low = y_at % 2

    def at_row(row):
        return (row % rows) * Y_SIZE + y_at

    partners = [(row_at * Y_SIZE + 2 * core + j, 2 * high + y_half) for j in range(2)]
    is_self = [(y_half == core) & (y_low == j) for j in range(2)]
    other = 2 * high + 1 - core
    after = {1: (at_row(row_at + core), other), 2: (at_row(row_at + 1), head)}
    before = {1: (at_row(row_at + rows - 1 + core), other), 2: (at_row(row_at + rows - 1), head)}
    sibling = (seq, other)
    across = (seq, 2 * (1 - high) + core)

    def x_peer(step):
        return (x_at + step) % X_SIZE

    def z_peer(step):
        return (z_at + step) % z_size

    def y_peer(step):
        return (y_at + step) % Y_SIZE

    def device(z, x, y):
        return ((z * X_SIZE + x) * Y_SIZE + y, head)

    barrier = pltpu.get_barrier_semaphore()

    def greet(target):
        pl.semaphore_signal(barrier, inc=1, device_id=target, device_id_type=MESH)

    for j in range(2):
        pl.when(jnp.logical_not(is_self[j]))(functools.partial(greet, partners[j]))
    for target in (after[1], after[2], before[1], before[2], sibling, across):
        greet(target)
    for step in range(1, X_SIZE):
        greet(device(z_at, x_peer(step), y_at))
    for step in range(1, z_size):
        greet(device(z_peer(step), x_at, y_at))
    for step in range(1, Y_SIZE):
        greet(device(z_at, x_at, y_peer(step)))

    def tiles_of(ref):
        return [ref[:, t * LANES : (t + 1) * LANES] for t in range(3)]

    to_pieces(tiles_of(k_ref), packs.at[K])
    to_pieces(tiles_of(q_ref), packs.at[Q], HEAD_DIM**-0.5)
    to_pieces(tiles_of(v_ref), packs.at[V])
    grads[head] = g_ref[...]

    greeted = X_SIZE + Y_SIZE + z_size - 3 + 8 - jnp.where(y_half == core, 1, 0)
    pl.semaphore_wait(barrier, greeted)

    started = []

    def remote(src, dst, send_sem, recv_sem, target):
        return pltpu.make_async_remote_copy(
            src_ref=src, dst_ref=dst, send_sem=send_sem, recv_sem=recv_sem, device_id=target, device_id_type=MESH
        )

    def send(*args):
        copy = remote(*args)
        copy.start()
        started.append(copy)
        return copy

    swap_waits = []

    def swap_start(kind, j, src, dst):
        copy = remote(src, dst, a2a_send_sems.at[kind, j], a2a_recv_sems.at[kind, y_low], partners[j])
        pl.when(jnp.logical_not(is_self[j]))(copy.start)
        pl.when(is_self[j])(pltpu.make_async_copy(src, dst, a2a_recv_sems.at[kind, y_low]).start)
        swap_waits.append((j, copy))

    def swap_wait(kind, j, dst):
        remote(dst, dst, a2a_send_sems.at[kind, j], a2a_recv_sems.at[kind, j], partners[j]).wait_recv()

    def grad_send(index, step, target):
        return send(grads.at[index], grads.at[index], grad_send_sems.at[step - 1], grad_recv_sems.at[step - 1], target)

    own = head
    own_across = 2 * (1 - high) + core
    from_step = {1: other, 2: own_across, 3: 2 * (1 - high) + 1 - core}

    def grad_wait(step):
        slot = grads.at[from_step[step]]
        remote(slot, slot, grad_send_sems.at[step - 1], grad_recv_sems.at[step - 1], across).wait_recv()

    grad_send(own, 2, across)
    for j in range(2):
        swap_start(K, j, packs.at[K, j], k_in.at[4 + y_low])
    grad_send(own, 1, sibling)
    for j in range(2):
        swap_start(Q, j, packs.at[Q, j], q_in.at[y_low])
    for j in range(2):
        swap_start(V, j, packs.at[V, j], v_in.at[4 + y_low])

    def flow(kind, buffer):
        for j in range(2):
            swap_wait(kind, j, buffer.at[4 + j])
            at = 0 if kind == K else 1
            for far in (2, 1):
                send(
                    buffer.at[4 + j],
                    buffer.at[4 - 2 * far + j],
                    flow_send_sems.at[at, far - 1, j],
                    flow_recv_sems.at[at, far - 1, j],
                    after[far],
                )

    def flow_wait(kind, buffer, far, j):
        at = 0 if kind == K else 1
        slot = buffer.at[4 - 2 * far + j]
        remote(
            slot, slot, flow_send_sems.at[at, far - 1, j], flow_recv_sems.at[at, far - 1, j], before[far]
        ).wait_recv()

    def spread(buffer, natural, turned, slot):
        first = buffer[slot, :SPAN]
        third = unfold(buffer[slot, SPAN:])
        natural[0, slot] = first
        natural[1, slot] = third.astype(BF16)
        turned[0, slot] = first.astype(F32).T.astype(BF16)
        turned[1, slot] = third.T.astype(BF16)

    def turn(buffer, turned, j):
        first = buffer[j, :SPAN].astype(F32).T
        third = unfold(buffer[j, SPAN:]).T
        upper = lax.broadcasted_iota(jnp.int32, (LANES, SPAN), 0) < HEAD_DIM
        turned[3 * j] = jnp.where(upper, first, 0.0).astype(BF16)
        turned[3 * j + 1] = jnp.where(upper, 0.0, first).astype(BF16)
        turned[3 * j + 2] = jnp.where(upper, third, 0.0).astype(BF16)

    flow(K, k_in)
    grad_wait(2)
    grad_send(own_across, 3, sibling)
    flow(V, v_in)
    for slot in (4, 5):
        spread(k_in, k_nat, k_tr, slot)
    for j in range(2):
        swap_wait(Q, j, q_in.at[j])
        turn(q_in, q_tr, j)
    for slot in (4, 5):
        spread(v_in, v_nat, v_tr, slot)
    grad_wait(1)
    grad_wait(3)
    acc = product(grads[0], w_ref[0:COLS], NN)
    for index in range(1, HEAD_SIZE):
        acc += product(grads[index], w_ref[index * COLS : (index + 1) * COLS], NN)
    to_pieces([acc[:, t * LANES : (t + 1) * LANES] for t in range(3)], packs.at[DO])
    for j in range(2):
        swap_start(DO, j, packs.at[DO, j], do_in.at[y_low])
    for index in range(HEAD_SIZE):
        grads_t[index] = grads[index].astype(F32).T.astype(BF16)
    for far in (1, 2):
        for j in range(2):
            flow_wait(K, k_in, far, j)
            spread(k_in, k_nat, k_tr, 4 - 2 * far + j)
    for far in (1, 2):
        for j in range(2):
            flow_wait(V, v_in, far, j)
            spread(v_in, v_nat, v_tr, 4 - 2 * far + j)

    def seen(slot):
        return (row_at > 0) | (slot >= 4 - 2 * core)

    def place(i, h):
        return h // 2, pl.multiple_of((h % 2) * HEAD_DIM, HEAD_DIM), 3 * i + h

    def forward_unit(i, h):
        tile, first, unit = place(i, h)
        query = q_tr[unit]
        top = None
        for j in range(WINDOW):
            block = product(k_nat[tile, i + j], query, NN)
            block = jnp.where(seen(i + j), block, -1e30)
            scores[j] = block
            peak = jnp.max(block, axis=0, keepdims=True)
            top = peak if top is None else jnp.maximum(top, peak)
        total = jnp.zeros((1, SPAN), F32)
        acc = jnp.zeros((HEAD_DIM, SPAN), F32)
        for j in range(WINDOW):
            part = jnp.exp(scores[j] - top)
            total += jnp.sum(part, axis=0, keepdims=True)
            part = part.astype(BF16)
            weights[unit, j] = part
            acc += product(v_tr[tile, i + j, pl.ds(first, HEAD_DIM), :], part, NN)
        share = 1.0 / total
        inverse[unit] = share
        att_tr[i, tile, pl.ds(first, HEAD_DIM), :] = acc * share

    def pack_turned(turned, kind, i):
        packs[kind, i, :SPAN] = turned[i, 0].T.astype(BF16)
        packs[kind, i, SPAN:] = fold(turned[i, 1].T).astype(BF16)

    for i in range(2):
        att_tr[i, 1] = jnp.zeros((LANES, SPAN), F32)
        dq_tr[i, 1] = jnp.zeros((LANES, SPAN), F32)
    dk_acc[...] = jnp.zeros(dk_acc.shape, F32)
    dv_acc[...] = jnp.zeros(dv_acc.shape, F32)

    for i in range(2):
        pl.loop(0, 3)(functools.partial(forward_unit, i))
        pack_turned(att_tr, ATT, i)
        swap_start(ATT, i, packs.at[ATT, i], att_in.at[y_low])

    def backward_unit(i, h):
        tile, first, unit = place(i, h)
        query = q_tr[unit]
        d_out = (do_tr[unit].astype(F32) * inverse[unit]).astype(BF16)
        do_tr[unit] = d_out
        d_half = do_tr[unit, pl.ds(first, HEAD_DIM), :].astype(F32)
        att_half = att_tr[i, tile, pl.ds(first, HEAD_DIM), :].astype(BF16).astype(F32)
        delta = jnp.sum(d_half * att_half, axis=0, keepdims=True)
        acc = jnp.zeros((HEAD_DIM, SPAN), F32)
        for j in range(WINDOW):
            part = weights[unit, j]
            d_part = product(v_nat[tile, i + j], d_out, NN)
            d_score = (part.astype(F32) * (d_part - delta)).astype(BF16)
            dk_acc[tile, i + j] += product(d_score, query, NT)
            dv_acc[tile, i + j] += product(part, d_out, NT)
            acc += product(k_tr[tile, i + j, pl.ds(first, HEAD_DIM), :], d_score, NN)
        dq_tr[i, tile, pl.ds(first, HEAD_DIM), :] = acc * (HEAD_DIM**-0.5)

    for j in range(2):
        swap_wait(DO, j, do_in.at[j])
        turn(do_in, do_tr, j)
    pl.loop(0, 3)(functools.partial(backward_unit, 0))
    pack_turned(dq_tr, DQ, 0)
    swap_start(DQ, 0, packs.at[DQ, 0], dq_in.at[y_low])

    for j in range(2):
        swap_wait(ATT, j, att_in.at[j])
    from_pieces(att_in, attended)
    att = attended[...]

    def projection(index):
        weight = w_ref[pl.ds(pl.multiple_of(index * COLS, COLS), COLS), :]
        return product(att, weight, NT)

    for at, index in enumerate((2 * (1 - high) + 1 - core, 2 * high + 1 - core)):
        proj_send[at] = projection(index).astype(BF16)
        send(proj_send.at[at], proj_in.at[at], proj_send_sems.at[at], proj_recv_sems.at[at], sibling)
    for index in range(HEAD_SIZE):
        term = product(grads_t[index], att, NN).astype(BF16)
        per_z = X_SIZE * terms.shape[2]
        for part in range(COLS // per_z):
            for x in range(X_SIZE):
                start = part * per_z + x * terms.shape[2]
                terms[index * (COLS // per_z) + part, x] = term[start : start + terms.shape[2]]
    x_copies = []
    for step in range(1, X_SIZE):
        x_copies.append(
            send(
                terms.at[:, x_peer(step)],
                x_in.at[step - 1],
                x_sems.at[0, step - 1],
                x_sems.at[1, step - 1],
                device(z_at, x_peer(step), y_at),
            )
        )
    proj_keep[0] = projection(own_across)
    proj_keep[1] = projection(own)

    pl.loop(0, 3)(functools.partial(backward_unit, 1))
    pack_turned(dq_tr, DQ, 1)
    swap_start(DQ, 1, packs.at[DQ, 1], dq_in.at[y_low])

    accs = (dk_acc, dv_acc)
    for at in range(2):
        for far in (2, 1):
            for j in range(2):
                slot = 4 - 2 * far + j
                back_send[at, slot, :SPAN] = accs[at][0, slot].astype(BF16)
                back_send[at, slot, SPAN:] = fold(accs[at][1, slot]).astype(BF16)
                send(
                    back_send.at[at, slot],
                    back_in.at[at, far - 1, j],
                    back_send_sems.at[at, far - 1, j],
                    back_recv_sems.at[at, far - 1, j],
                    before[far],
                )

    remote(proj_send.at[0], proj_in.at[0], proj_send_sems.at[0], proj_recv_sems.at[0], sibling).wait_recv()
    hip_send[...] = (proj_keep[0] + proj_in[0].astype(F32)).astype(BF16)
    hip_copy = send(hip_send, hip_in, proj_send_sems.at[2], proj_recv_sems.at[2], across)

    for copy in x_copies:
        copy.wait_recv()
    for z in range(z_size):
        total = terms[z, x_at].astype(F32)
        for step in range(1, X_SIZE):
            total += x_in[step - 1, z].astype(F32)
        z_send[z] = total.astype(BF16)
    z_copies = []
    for step in range(1, z_size):
        z_copies.append(
            send(
                z_send.at[z_peer(step)],
                z_in.at[step - 1],
                z_sems.at[0, step - 1],
                z_sems.at[1, step - 1],
                device(z_peer(step), x_at, y_at),
            )
        )

    for at in range(2):
        for j in range(2):
            tile = accs[at][0, 4 + j]
            third = fold(accs[at][1, 4 + j])
            for far in (1, 2):
                piece = back_in.at[at, far - 1, j]
                remote(
                    piece, piece, back_send_sems.at[at, far - 1, j], back_recv_sems.at[at, far - 1, j], after[far]
                ).wait_recv()
                tile += back_in[at, far - 1, j, :SPAN].astype(F32)
                third += back_in[at, far - 1, j, SPAN:].astype(F32)
            kind = (DK, DV)[at]
            packs[kind, j, :SPAN] = tile.astype(BF16)
            packs[kind, j, SPAN:] = third.astype(BF16)
            swap_start(kind, j, packs.at[kind, j], (dk_in, dv_in)[at].at[y_low])

    for copy in z_copies:
        copy.wait_recv()
    sums[...] = z_send[z_at].astype(F32)
    for step in range(1, z_size):
        sums[...] += z_in[step - 1].astype(F32)
    out_rows = dw_ref.shape[0]
    for piece in range(Y_SIZE):
        y_send[piece, 0:out_rows] = sums[piece * out_rows : (piece + 1) * out_rows]
    y_copies = []
    for step in range(1, Y_SIZE):
        y_copies.append(
            send(
                y_send.at[y_peer(step)],
                y_in.at[step - 1],
                y_sems.at[0, step - 1],
                y_sems.at[1, step - 1],
                device(z_at, x_at, y_peer(step)),
            )
        )

    for j in range(2):
        swap_wait(DQ, j, dq_in.at[j])
    from_pieces(dq_in, dq_ref)
    remote(proj_send.at[1], proj_in.at[1], proj_send_sems.at[1], proj_recv_sems.at[1], sibling).wait_recv()
    hip_copy.wait_recv()
    proj_ref[...] = (proj_keep[1] + proj_in[1].astype(F32) + hip_in[...].astype(F32)).astype(BF16)
    for j in range(2):
        swap_wait(DK, j, dk_in.at[j])
    from_pieces(dk_in, dk_ref)
    for j in range(2):
        swap_wait(DV, j, dv_in.at[j])
    from_pieces(dv_in, dv_ref)
    result = y_send[y_at]
    for step in range(1, Y_SIZE):
        y_copies[step - 1].wait_recv()
        result += y_in[step - 1]
    dw_ref[...] = result[0:out_rows]

    for copy in started:
        copy.wait_send()
    for j, copy in swap_waits:
        pl.when(jnp.logical_not(is_self[j]))(copy.wait_send)


def shards(query_rows, key_rows, value_rows, out_weight, out_grad):
    seq_size = lax.axis_size("seq")
    z_size = seq_size // (X_SIZE * Y_SIZE)
    out_rows = out_weight.shape[0] // seq_size
    block = out_rows * Y_SIZE
    padded = (out_rows + 7) // 8 * 8
    rows_out = jax.ShapeDtypeStruct((SPAN, COLS), BF16)
    vmem = pltpu.VMEM
    dma = pltpu.SemaphoreType.DMA
    piece = (PIECE, LANES)
    scratch = [
        vmem((8, 2) + piece, BF16),
        vmem((2,) + piece, BF16),
        vmem((2,) + piece, BF16),
        vmem((SLOTS,) + piece, BF16),
        vmem((SLOTS,) + piece, BF16),
        vmem((2,) + piece, BF16),
        vmem((2,) + piece, BF16),
        vmem((2,) + piece, BF16),
        vmem((2,) + piece, BF16),
        vmem((HEAD_SIZE, SPAN, COLS), BF16),
        vmem((HEAD_SIZE, COLS, SPAN), BF16),
        vmem((2, SLOTS, SPAN, LANES), BF16),
        vmem((2, SLOTS, SPAN, LANES), BF16),
        vmem((2, SLOTS, LANES, SPAN), BF16),
        vmem((2, SLOTS, LANES, SPAN), BF16),
        vmem((6, LANES, SPAN), BF16),
        vmem((6, LANES, SPAN), BF16),
        vmem((WINDOW, SPAN, SPAN), F32),
        vmem((6, WINDOW, SPAN, SPAN), BF16),
        vmem((6, 1, SPAN), F32),
        vmem((2, 2, LANES, SPAN), F32),
        vmem((2, 2, LANES, SPAN), F32),
        vmem((2, SLOTS, SPAN, LANES), F32),
        vmem((2, SLOTS, SPAN, LANES), F32),
        vmem((2, 4) + piece, BF16),
        vmem((2, 2, 2) + piece, BF16),
        vmem((SPAN, COLS), BF16),
        vmem((2, SPAN, COLS), BF16),
        vmem((2, SPAN, COLS), BF16),
        vmem((2, SPAN, COLS), F32),
        vmem((SPAN, COLS), BF16),
        vmem((SPAN, COLS), BF16),
        vmem((z_size, X_SIZE, block, COLS), BF16),
        vmem((X_SIZE - 1, z_size, block, COLS), BF16),
        vmem((z_size, block, COLS), BF16),
        vmem((z_size - 1, block, COLS), BF16),
        vmem((Y_SIZE, padded, COLS), F32),
        vmem((Y_SIZE - 1, padded, COLS), F32),
        vmem((block, COLS), F32),
        dma((8, 2)),
        dma((8, 2)),
        dma((2, 2, 2)),
        dma((2, 2, 2)),
        dma((2, 2, 2)),
        dma((2, 2, 2)),
        dma((3,)),
        dma((3,)),
        dma((3,)),
        dma((3,)),
        dma((2, X_SIZE - 1)),
        dma((2, z_size - 1)),
        dma((2, Y_SIZE - 1)),
    ]
    return pl.pallas_call(
        functools.partial(layer_kernel, z_size),
        out_shape=(rows_out,) * 4 + (jax.ShapeDtypeStruct((out_rows, COLS), F32),),
        in_specs=[pl.BlockSpec(memory_space=pltpu.VMEM)] * 5,
        out_specs=(pl.BlockSpec(memory_space=pltpu.VMEM),) * 5,
        scratch_shapes=scratch,
        compiler_params=pltpu.CompilerParams(
            collective_id=0, has_side_effects=True, vmem_limit_bytes=48 * 1024 * 1024
        ),
    )(query_rows, key_rows, value_rows, out_weight, out_grad)


def solution(mesh):
    in_specs = (
        P("seq", "head"),
        P("seq", "head"),
        P("seq", "head"),
        P(None, "head"),
        P("seq", "head"),
    )
    out_specs = (
        P("seq", "head"),
        P("seq", "head"),
        P("seq", "head"),
        P("seq", "head"),
        P("seq", "head"),
    )
    return jax.shard_map(shards, mesh=mesh, in_specs=in_specs, out_specs=out_specs, check_vma=False)
```

```python
import functools

import jax
import jax.numpy as jnp
from jax import lax
from jax.experimental import pallas as pl
from jax.experimental.pallas import tpu as pltpu
from jax.sharding import PartitionSpec as P

MESH = pl.DeviceIdType.MESH
BF16 = jnp.bfloat16
F32 = jnp.float32
SPAN = 256
COLS = 384
HEAD_DIM = 64
LANES = 128
HALF = 128
PIECE = SPAN + HALF
SLOTS = 6
WINDOW = 5
X_SIZE = 4
Y_SIZE = 4
HEAD_SIZE = 4
NN = (((1,), (0,)), ((), ()))
NT = (((1,), (1,)), ((), ()))
K, Q, V, DO, ATT, DQ, DK, DV = range(8)


def product(left, right, dims):
    return lax.dot_general(left, right, dims, preferred_element_type=F32)


def low_lanes(rows):
    return lax.broadcasted_iota(jnp.int32, (rows, LANES), 1) < HEAD_DIM


def swap(block):
    return pltpu.roll(block, HEAD_DIM, 1)


def fold(block):
    return jnp.where(low_lanes(HALF), block[:HALF], swap(block[HALF:]))


def to_pieces(tiles, piece_ref, scale=None):
    first, middle, last = [tile.astype(F32) for tile in tiles]
    if scale is not None:
        first, middle, last = first * scale, middle * scale, last * scale
    swapped = swap(middle)
    piece_ref[0, :SPAN] = first.astype(BF16)
    piece_ref[0, SPAN:] = jnp.where(low_lanes(HALF), middle[:HALF], swapped[HALF:]).astype(BF16)
    piece_ref[1, :SPAN] = last.astype(BF16)
    piece_ref[1, SPAN:] = jnp.where(low_lanes(HALF), swapped[:HALF], middle[HALF:]).astype(BF16)


def from_pieces(piece_ref, out_ref):
    out_ref[:, 0:LANES] = piece_ref[0, :SPAN]
    out_ref[:, 2 * LANES : 3 * LANES] = piece_ref[1, :SPAN]
    low = piece_ref[0, SPAN:].astype(F32)
    high = piece_ref[1, SPAN:].astype(F32)
    top = jnp.where(low_lanes(HALF), low, swap(high))
    bottom = jnp.where(low_lanes(HALF), swap(low), high)
    out_ref[:HALF, LANES : 2 * LANES] = top.astype(BF16)
    out_ref[HALF:, LANES : 2 * LANES] = bottom.astype(BF16)


def unfold(third):
    wide = third.astype(F32)
    return jnp.concatenate([wide, swap(wide)], axis=0)


def layer_kernel(
    z_size,
    q_hbm, k_hbm, v_hbm, w_hbm, g_hbm,
    proj_out, dq_out, dk_out, dv_out, dw_out,
    proj_ref, dq_ref, dk_ref, dv_ref, dw_ref,
    q_ref, k_ref, v_ref, w_ref, packs, q_in, do_in, k_in, v_in, att_in, dq_in, dk_in, dv_in,
    grads, grads_t, k_nat, v_nat, k_tr, v_tr, q_tr, do_tr,
    scores, weights, inverse, att_tr, dq_tr, dk_acc, dv_acc,
    near_send, near_in, back_send, back_in, attended,
    proj_send, proj_in, proj_keep, hip_send, hip_in,
    x_terms, x_in, z_send, z_in, z_terms, z_first_in, x_send, x_last_in, y_send, y_in, sums,
    load_sems, store_sems, a2a_send_sems, a2a_recv_sems, flow_sems, near_sems, back_sems, term_sems,
    grad_send_sems, grad_recv_sems, proj_send_sems, proj_recv_sems, x_sems, z_sems, z_first_sems, x_last_sems, y_sems,
):
    seq = lax.axis_index("seq")
    head = lax.axis_index("head")
    rows = z_size * X_SIZE
    y_at = seq % Y_SIZE
    row_at = seq // Y_SIZE
    x_at = row_at % X_SIZE
    z_at = row_at // X_SIZE
    core = head % 2
    high = head // 2
    y_half = y_at // 2
    y_low = y_at % 2

    def at_row(row):
        return (row % rows) * Y_SIZE + y_at

    partners = [(row_at * Y_SIZE + 2 * core + j, 2 * high + y_half) for j in range(2)]
    is_self = [(y_half == core) & (y_low == j) for j in range(2)]
    other = 2 * high + 1 - core
    after = (at_row(row_at + 1), head)
    before = (at_row(row_at + rows - 1), head)
    sibling = (seq, other)
    across = (seq, 2 * (1 - high) + core)

    def x_peer(step):
        return (x_at + step) % X_SIZE

    def z_peer(step):
        return (z_at + step) % z_size

    def y_peer(step):
        return (y_at + step) % Y_SIZE

    def device(z, x, y):
        return ((z * X_SIZE + x) * Y_SIZE + y, head)

    barrier = pltpu.get_barrier_semaphore()

    def greet(target):
        pl.semaphore_signal(barrier, inc=1, device_id=target, device_id_type=MESH)

    for j in range(2):
        pl.when(jnp.logical_not(is_self[j]))(functools.partial(greet, partners[j]))
    for target in (after, before, sibling, across):
        greet(target)
    for step in range(1, X_SIZE):
        greet(device(z_at, x_peer(step), y_at))
    for step in range(1, z_size):
        greet(device(z_peer(step), x_at, y_at))
    for step in range(1, Y_SIZE):
        greet(device(z_at, x_at, y_peer(step)))

    def tiles_of(ref):
        return [ref[:, t * LANES : (t + 1) * LANES] for t in range(3)]

    loads = {}
    for at, (name, src, dst) in enumerate(
        (("k", k_hbm, k_ref), ("v", v_hbm, v_ref), ("q", q_hbm, q_ref), ("g", g_hbm, grads.at[head]), ("w", w_hbm, w_ref))
    ):
        loads[name] = pltpu.make_async_copy(src, dst, load_sems.at[at])
        loads[name].start()
    loads["k"].wait()
    to_pieces(tiles_of(k_ref), packs.at[K])
    loads["v"].wait()
    to_pieces(tiles_of(v_ref), packs.at[V])
    loads["q"].wait()
    to_pieces(tiles_of(q_ref), packs.at[Q], HEAD_DIM**-0.5)
    loads["g"].wait()

    greeted = X_SIZE + Y_SIZE + z_size - 3 + 6 - jnp.where(y_half == core, 1, 0)
    pl.semaphore_wait(barrier, greeted)

    started = []
    stores = []

    def store(src, dst):
        copy = pltpu.make_async_copy(src, dst, store_sems.at[len(stores)])
        copy.start()
        stores.append(copy)


    def remote(src, dst, send_sem, recv_sem, target):
        return pltpu.make_async_remote_copy(
            src_ref=src, dst_ref=dst, send_sem=send_sem, recv_sem=recv_sem, device_id=target, device_id_type=MESH
        )

    def send(*args):
        copy = remote(*args)
        copy.start()
        started.append(copy)
        return copy

    swap_waits = []

    def swap_start(kind, j, src, dst):
        copy = remote(src, dst, a2a_send_sems.at[kind, j], a2a_recv_sems.at[kind, y_low], partners[j])
        pl.when(jnp.logical_not(is_self[j]))(copy.start)
        pl.when(is_self[j])(pltpu.make_async_copy(src, dst, a2a_recv_sems.at[kind, y_low]).start)
        swap_waits.append((j, copy))

    def swap_wait(kind, j, dst):
        remote(dst, dst, a2a_send_sems.at[kind, j], a2a_recv_sems.at[kind, j], partners[j]).wait_recv()

    def grad_send(index, step, target):
        return send(grads.at[index], grads.at[index], grad_send_sems.at[step - 1], grad_recv_sems.at[step - 1], target)

    own = head
    own_across = 2 * (1 - high) + core
    from_step = {1: other, 2: own_across, 3: 2 * (1 - high) + 1 - core}

    def grad_wait(step):
        slot = grads.at[from_step[step]]
        remote(slot, slot, grad_send_sems.at[step - 1], grad_recv_sems.at[step - 1], across).wait_recv()

    for kind, buffer in ((K, k_in), (V, v_in)):
        for j in range(2):
            swap_start(kind, j, packs.at[kind, j], buffer.at[4 + y_low])
    for j in range(2):
        swap_start(Q, j, packs.at[Q, j], q_in.at[y_low])

    def near_copy(at, buffer, slot, j):
        return remote(
            buffer.at[slot + j], buffer.at[2 + j], near_sems.at[0, at, j], near_sems.at[1, at, j], sibling
        )

    def far_copy(at, buffer, j):
        return remote(buffer.at[4 + j], buffer.at[j], flow_sems.at[0, at, j], flow_sems.at[1, at, j], after)

    def flow(at, kind, buffer):
        for j in range(2):
            swap_wait(kind, j, buffer.at[4 + j])
            copy = far_copy(at, buffer, j)
            copy.start()
            started.append(copy)
            near = near_copy(at, buffer, 4, j)
            pl.when(core == 0)(near.start)
            started.append(near)

    def flow_on(at, buffer):
        for j in range(2):
            remote(buffer.at[j], buffer.at[j], flow_sems.at[0, at, j], flow_sems.at[1, at, j], before).wait_recv()
            pl.when(core == 1)(near_copy(at, buffer, 0, j).start)

    def near_wait(at, buffer):
        for j in range(2):
            near_copy(at, buffer, 2, j).wait_recv()

    def spread(buffer, natural, turned, slot):
        first = buffer[slot, :SPAN]
        third = unfold(buffer[slot, SPAN:])
        natural[0, slot] = first
        natural[1, slot] = third.astype(BF16)
        turned[0, slot] = first.astype(F32).T.astype(BF16)
        turned[1, slot] = third.T.astype(BF16)

    def turn(buffer, turned, j):
        first = buffer[j, :SPAN].astype(F32).T
        third = unfold(buffer[j, SPAN:]).T
        upper = lax.broadcasted_iota(jnp.int32, (LANES, SPAN), 0) < HEAD_DIM
        turned[3 * j] = jnp.where(upper, first, 0.0).astype(BF16)
        turned[3 * j + 1] = jnp.where(upper, 0.0, first).astype(BF16)
        turned[3 * j + 2] = jnp.where(upper, third, 0.0).astype(BF16)

    flow(0, K, k_in)
    flow(1, V, v_in)
    grad_send(own, 2, across)
    grad_send(own, 1, sibling)
    for slot in (4, 5):
        spread(k_in, k_nat, k_tr, slot)
        spread(v_in, v_nat, v_tr, slot)
    for j in range(2):
        swap_wait(Q, j, q_in.at[j])
        turn(q_in, q_tr, j)
    flow_on(0, k_in)
    for slot in (0, 1):
        spread(k_in, k_nat, k_tr, slot)
    flow_on(1, v_in)
    near_wait(0, k_in)
    for slot in (2, 3):
        spread(k_in, k_nat, k_tr, slot)
    for slot in (0, 1):
        spread(v_in, v_nat, v_tr, slot)
    near_wait(1, v_in)
    for slot in (2, 3):
        spread(v_in, v_nat, v_tr, slot)

    def seen(slot):
        return (row_at > 0) | (slot >= 4 - 2 * core)

    def place(i, h):
        return h // 2, pl.multiple_of((h % 2) * HEAD_DIM, HEAD_DIM), 3 * i + h

    def forward_unit(i, h):
        tile, first, unit = place(i, h)
        query = q_tr[unit]
        top = None
        for j in range(WINDOW):
            block = product(k_nat[tile, i + j], query, NN)
            block = jnp.where(seen(i + j), block, -1e30)
            scores[j] = block
            peak = jnp.max(block, axis=0, keepdims=True)
            top = peak if top is None else jnp.maximum(top, peak)
        total = jnp.zeros((1, SPAN), F32)
        acc = jnp.zeros((HEAD_DIM, SPAN), F32)
        for j in range(WINDOW):
            part = jnp.exp(scores[j] - top)
            total += jnp.sum(part, axis=0, keepdims=True)
            part = part.astype(BF16)
            weights[unit, j] = part
            acc += product(v_tr[tile, i + j, pl.ds(first, HEAD_DIM), :], part, NN)
        share = 1.0 / total
        inverse[unit] = share
        att_tr[i, tile, pl.ds(first, HEAD_DIM), :] = acc * share

    def pack_turned(turned, kind, i):
        packs[kind, i, :SPAN] = turned[i, 0].T.astype(BF16)
        packs[kind, i, SPAN:] = fold(turned[i, 1].T).astype(BF16)

    for i in range(2):
        att_tr[i, 1] = jnp.zeros((LANES, SPAN), F32)
        dq_tr[i, 1] = jnp.zeros((LANES, SPAN), F32)
    dk_acc[...] = jnp.zeros(dk_acc.shape, F32)
    dv_acc[...] = jnp.zeros(dv_acc.shape, F32)

    def forward(i):
        pl.loop(0, 3)(functools.partial(forward_unit, i))
        pack_turned(att_tr, ATT, i)
        swap_start(ATT, i, packs.at[ATT, i], att_in.at[y_low])

    forward(0)
    grad_wait(2)
    grad_send(own_across, 3, sibling)
    forward(1)
    loads["w"].wait()
    grad_wait(1)
    grad_wait(3)
    acc = product(grads[0], w_ref[0:COLS], NN)
    for index in range(1, HEAD_SIZE):
        acc += product(grads[index], w_ref[index * COLS : (index + 1) * COLS], NN)
    to_pieces([acc[:, t * LANES : (t + 1) * LANES] for t in range(3)], packs.at[DO])
    for j in range(2):
        swap_start(DO, j, packs.at[DO, j], do_in.at[y_low])
    for index in range(HEAD_SIZE):
        grads_t[index] = grads[index].astype(F32).T.astype(BF16)

    def backward_unit(i, h):
        tile, first, unit = place(i, h)
        query = q_tr[unit]
        d_out = (do_tr[unit].astype(F32) * inverse[unit]).astype(BF16)
        do_tr[unit] = d_out
        d_half = do_tr[unit, pl.ds(first, HEAD_DIM), :].astype(F32)
        att_half = att_tr[i, tile, pl.ds(first, HEAD_DIM), :].astype(BF16).astype(F32)
        delta = jnp.sum(d_half * att_half, axis=0, keepdims=True)
        acc = jnp.zeros((HEAD_DIM, SPAN), F32)
        for j in range(WINDOW):
            part = weights[unit, j]
            d_part = product(v_nat[tile, i + j], d_out, NN)
            d_score = (part.astype(F32) * (d_part - delta)).astype(BF16)
            dk_acc[tile, i + j] += product(d_score, query, NT)
            dv_acc[tile, i + j] += product(part, d_out, NT)
            acc += product(k_tr[tile, i + j, pl.ds(first, HEAD_DIM), :], d_score, NN)
        dq_tr[i, tile, pl.ds(first, HEAD_DIM), :] = acc * (HEAD_DIM**-0.5)

    for j in range(2):
        swap_wait(ATT, j, att_in.at[j])
    from_pieces(att_in, attended)
    att = attended[...]

    def projection(index):
        weight = w_ref[pl.ds(pl.multiple_of(index * COLS, COLS), COLS), :]
        return product(att, weight, NT)

    block = x_terms.shape[2]
    x_cols = x_terms.shape[3]
    per_z = X_SIZE * block
    for index in range(HEAD_SIZE):
        term = product(grads_t[index], att, NN).astype(BF16)
        for part in range(COLS // per_z):
            for x in range(X_SIZE):
                start = part * per_z + x * block
                z = index * (COLS // per_z) + part
                x_terms[z, x] = term[start : start + block, :x_cols]
                z_terms[z, x] = term[start : start + block, x_cols:]
    x_copies = []
    for step in range(1, X_SIZE):
        x_copies.append(
            send(
                x_terms.at[:, x_peer(step)],
                x_in.at[step - 1],
                x_sems.at[0, step - 1],
                x_sems.at[1, step - 1],
                device(z_at, x_peer(step), y_at),
            )
        )
    z_first_copies = []
    for step in range(1, z_size):
        z_first_copies.append(
            send(
                z_terms.at[z_peer(step)],
                z_first_in.at[step - 1],
                z_first_sems.at[0, step - 1],
                z_first_sems.at[1, step - 1],
                device(z_peer(step), x_at, y_at),
            )
        )
    for at, index in enumerate((2 * (1 - high) + 1 - core, 2 * high + 1 - core)):
        proj_send[at] = projection(index).astype(BF16)
        send(proj_send.at[at], proj_in.at[at], proj_send_sems.at[at], proj_recv_sems.at[at], sibling)
    proj_keep[0] = projection(own_across)
    proj_keep[1] = projection(own)

    for j in range(2):
        swap_wait(DO, j, do_in.at[j])
        turn(do_in, do_tr, j)
    for i in range(2):
        pl.loop(0, 3)(functools.partial(backward_unit, i))
        pack_turned(dq_tr, DQ, i)
        swap_start(DQ, i, packs.at[DQ, i], dq_in.at[y_low])
        if i == 0:
            remote(proj_send.at[0], proj_in.at[0], proj_send_sems.at[0], proj_recv_sems.at[0], sibling).wait_recv()
            hip_send[...] = (proj_keep[0] + proj_in[0].astype(F32)).astype(BF16)
            hip_copy = send(hip_send, hip_in, proj_send_sems.at[2], proj_recv_sems.at[2], across)

    accs = (dk_acc, dv_acc)

    def term_copy(at, j):
        return remote(
            near_send.at[at, j], near_in.at[at, j], term_sems.at[0, at, j], term_sems.at[1, at, j], sibling
        )

    def back_copy(at, j, target):
        return remote(
            back_send.at[at, j], back_in.at[at, j], back_sems.at[0, at, j], back_sems.at[1, at, j], target
        )

    def send_back(summed):
        for at in range(2):
            for j in range(2):
                tile = accs[at][0, j]
                third = fold(accs[at][1, j])
                if summed:
                    term_copy(at, j).wait_recv()
                    tile += near_in[at, j, :SPAN].astype(F32)
                    third += near_in[at, j, SPAN:].astype(F32)
                back_send[at, j, :SPAN] = tile.astype(BF16)
                back_send[at, j, SPAN:] = third.astype(BF16)
                back_copy(at, j, before).start()

    for at in range(2):
        for j in range(2):
            near_send[at, j, :SPAN] = accs[at][0, 2 + j].astype(BF16)
            near_send[at, j, SPAN:] = fold(accs[at][1, 2 + j]).astype(BF16)
            copy = term_copy(at, j)
            copy.start()
            started.append(copy)
            started.append(back_copy(at, j, before))
    pl.when(core == 0)(functools.partial(send_back, False))
    pl.when(core == 1)(functools.partial(send_back, True))

    for copy in x_copies:
        copy.wait_recv()
    for z in range(z_size):
        total = x_terms[z, x_at].astype(F32)
        for step in range(1, X_SIZE):
            total += x_in[step - 1, z].astype(F32)
        z_send[z] = total.astype(BF16)
    z_copies = []
    for step in range(1, z_size):
        z_copies.append(
            send(
                z_send.at[z_peer(step)],
                z_in.at[step - 1],
                z_sems.at[0, step - 1],
                z_sems.at[1, step - 1],
                device(z_peer(step), x_at, y_at),
            )
        )
    for copy in z_first_copies:
        copy.wait_recv()
    for x in range(X_SIZE):
        total = z_terms[z_at, x].astype(F32)
        for step in range(1, z_size):
            total += z_first_in[step - 1, x].astype(F32)
        x_send[x] = total.astype(BF16)
    x_last_copies = []
    for step in range(1, X_SIZE):
        x_last_copies.append(
            send(
                x_send.at[x_peer(step)],
                x_last_in.at[step - 1],
                x_last_sems.at[0, step - 1],
                x_last_sems.at[1, step - 1],
                device(z_at, x_peer(step), y_at),
            )
        )

    def finish(near):
        for at in range(2):
            for j in range(2):
                tile = accs[at][0, 4 + j]
                third = fold(accs[at][1, 4 + j])
                if near:
                    term_copy(at, j).wait_recv()
                    tile += near_in[at, j, :SPAN].astype(F32)
                    third += near_in[at, j, SPAN:].astype(F32)
                back_copy(at, j, after).wait_recv()
                tile += back_in[at, j, :SPAN].astype(F32)
                third += back_in[at, j, SPAN:].astype(F32)
                kind = (DK, DV)[at]
                packs[kind, j, :SPAN] = tile.astype(BF16)
                packs[kind, j, SPAN:] = third.astype(BF16)
                swap_start(kind, j, packs.at[kind, j], (dk_in, dv_in)[at].at[y_low])

    finish_waits = len(swap_waits)
    pl.when(core == 0)(functools.partial(finish, True))
    del swap_waits[finish_waits:]
    pl.when(core == 1)(functools.partial(finish, False))
    del swap_waits[finish_waits:]
    for kind, buffer in ((DK, dk_in), (DV, dv_in)):
        for j in range(2):
            src = packs.at[kind, j]
            swap_waits.append(
                (j, remote(src, src, a2a_send_sems.at[kind, j], a2a_recv_sems.at[kind, y_low], partners[j]))
            )

    for copy in z_copies:
        copy.wait_recv()
    sums[:, :x_cols] = z_send[z_at].astype(F32)
    for step in range(1, z_size):
        sums[:, :x_cols] += z_in[step - 1].astype(F32)
    for copy in x_last_copies:
        copy.wait_recv()
    sums[:, x_cols:] = x_send[x_at].astype(F32)
    for step in range(1, X_SIZE):
        sums[:, x_cols:] += x_last_in[step - 1].astype(F32)
    out_rows = dw_ref.shape[0]
    for piece in range(Y_SIZE):
        y_send[piece, 0:out_rows] = sums[piece * out_rows : (piece + 1) * out_rows]
    y_copies = []
    for step in range(1, Y_SIZE):
        y_copies.append(
            send(
                y_send.at[y_peer(step)],
                y_in.at[step - 1],
                y_sems.at[0, step - 1],
                y_sems.at[1, step - 1],
                device(z_at, x_at, y_peer(step)),
            )
        )

    for j in range(2):
        swap_wait(DQ, j, dq_in.at[j])
    from_pieces(dq_in, dq_ref)
    store(dq_ref, dq_out)
    remote(proj_send.at[1], proj_in.at[1], proj_send_sems.at[1], proj_recv_sems.at[1], sibling).wait_recv()
    hip_copy.wait_recv()
    proj_ref[...] = (proj_keep[1] + proj_in[1].astype(F32) + hip_in[...].astype(F32)).astype(BF16)
    store(proj_ref, proj_out)
    for j in range(2):
        swap_wait(DK, j, dk_in.at[j])
    from_pieces(dk_in, dk_ref)
    store(dk_ref, dk_out)
    for j in range(2):
        swap_wait(DV, j, dv_in.at[j])
    from_pieces(dv_in, dv_ref)
    store(dv_ref, dv_out)
    result = y_send[y_at]
    for step in range(1, Y_SIZE):
        y_copies[step - 1].wait_recv()
        result += y_in[step - 1]
    dw_ref[...] = result[0:out_rows]
    store(dw_ref, dw_out)

    for copy in started:
        copy.wait_send()
    for j, copy in swap_waits:
        pl.when(jnp.logical_not(is_self[j]))(copy.wait_send)
    for copy in stores:
        copy.wait()


def results_kernel(*refs):
    sems = refs[-1]
    count = (len(refs) - 1) // 3
    sources, targets, held = refs[:count], refs[count : 2 * count], refs[2 * count : 3 * count]
    loads = [pltpu.make_async_copy(sources[at], held[at], sems.at[0, at]) for at in range(count)]
    stores = [pltpu.make_async_copy(held[at], targets[at], sems.at[1, at]) for at in range(count)]
    for copy in loads:
        copy.start()
    for load, copy in zip(loads, stores):
        load.wait()
        copy.start()
    for copy in stores:
        copy.wait()


def shards(query_rows, key_rows, value_rows, out_weight, out_grad):
    seq_size = lax.axis_size("seq")
    z_size = seq_size // (X_SIZE * Y_SIZE)
    out_rows = out_weight.shape[0] // seq_size
    block = out_rows * Y_SIZE
    padded = (out_rows + 7) // 8 * 8
    x_cols = 2 * LANES
    rows_out = jax.ShapeDtypeStruct((SPAN, COLS), BF16)
    vmem = pltpu.VMEM
    dma = pltpu.SemaphoreType.DMA
    piece = (PIECE, LANES)
    scratch = [
        vmem((SPAN, COLS), BF16),
        vmem((SPAN, COLS), BF16),
        vmem((SPAN, COLS), BF16),
        vmem((SPAN, COLS), BF16),
        vmem((out_rows, COLS), F32),
        vmem((SPAN, COLS), BF16),
        vmem((SPAN, COLS), BF16),
        vmem((SPAN, COLS), BF16),
        vmem(out_weight.shape, BF16),
        vmem((8, 2) + piece, BF16),
        vmem((2,) + piece, BF16),
        vmem((2,) + piece, BF16),
        vmem((SLOTS,) + piece, BF16),
        vmem((SLOTS,) + piece, BF16),
        vmem((2,) + piece, BF16),
        vmem((2,) + piece, BF16),
        vmem((2,) + piece, BF16),
        vmem((2,) + piece, BF16),
        vmem((HEAD_SIZE, SPAN, COLS), BF16),
        vmem((HEAD_SIZE, COLS, SPAN), BF16),
        vmem((2, SLOTS, SPAN, LANES), BF16),
        vmem((2, SLOTS, SPAN, LANES), BF16),
        vmem((2, SLOTS, LANES, SPAN), BF16),
        vmem((2, SLOTS, LANES, SPAN), BF16),
        vmem((6, LANES, SPAN), BF16),
        vmem((6, LANES, SPAN), BF16),
        vmem((WINDOW, SPAN, SPAN), F32),
        vmem((6, WINDOW, SPAN, SPAN), BF16),
        vmem((6, 1, SPAN), F32),
        vmem((2, 2, LANES, SPAN), F32),
        vmem((2, 2, LANES, SPAN), F32),
        vmem((2, SLOTS, SPAN, LANES), F32),
        vmem((2, SLOTS, SPAN, LANES), F32),
        vmem((2, 2) + piece, BF16),
        vmem((2, 2) + piece, BF16),
        vmem((2, 2) + piece, BF16),
        vmem((2, 2) + piece, BF16),
        vmem((SPAN, COLS), BF16),
        vmem((2, SPAN, COLS), BF16),
        vmem((2, SPAN, COLS), BF16),
        vmem((2, SPAN, COLS), F32),
        vmem((SPAN, COLS), BF16),
        vmem((SPAN, COLS), BF16),
        vmem((z_size, X_SIZE, block, x_cols), BF16),
        vmem((X_SIZE - 1, z_size, block, x_cols), BF16),
        vmem((z_size, block, x_cols), BF16),
        vmem((z_size - 1, block, x_cols), BF16),
        vmem((z_size, X_SIZE, block, COLS - x_cols), BF16),
        vmem((z_size - 1, X_SIZE, block, COLS - x_cols), BF16),
        vmem((X_SIZE, block, COLS - x_cols), BF16),
        vmem((X_SIZE - 1, block, COLS - x_cols), BF16),
        vmem((Y_SIZE, padded, COLS), F32),
        vmem((Y_SIZE - 1, padded, COLS), F32),
        vmem((block, COLS), F32),
        dma((5,)),
        dma((5,)),
        dma((8, 2)),
        dma((8, 2)),
        dma((2, 2, 2)),
        dma((2, 2, 2)),
        dma((2, 2, 2)),
        dma((2, 2, 2)),
        dma((3,)),
        dma((3,)),
        dma((3,)),
        dma((3,)),
        dma((2, X_SIZE - 1)),
        dma((2, z_size - 1)),
        dma((2, z_size - 1)),
        dma((2, X_SIZE - 1)),
        dma((2, Y_SIZE - 1)),
    ]
    outputs = (rows_out,) * 4 + (jax.ShapeDtypeStruct((out_rows, COLS), F32),)
    anywhere = pl.BlockSpec(memory_space=pl.ANY)
    results = pl.pallas_call(
        functools.partial(layer_kernel, z_size),
        out_shape=outputs,
        in_specs=[anywhere] * 5,
        out_specs=(anywhere,) * 5,
        scratch_shapes=scratch,
        compiler_params=pltpu.CompilerParams(
            collective_id=0, has_side_effects=True, vmem_limit_bytes=60 * 1024 * 1024
        ),
    )(query_rows, key_rows, value_rows, out_weight, out_grad)
    return pl.pallas_call(
        results_kernel,
        out_shape=outputs,
        in_specs=[anywhere] * 5,
        out_specs=(anywhere,) * 5,
        scratch_shapes=[vmem(kept.shape, kept.dtype) for kept in outputs] + [dma((2, 5))],
        compiler_params=pltpu.CompilerParams(vmem_limit_bytes=60 * 1024 * 1024),
    )(*results)


def solution(mesh):
    in_specs = (
        P("seq", "head"),
        P("seq", "head"),
        P("seq", "head"),
        P(None, "head"),
        P("seq", "head"),
    )
    out_specs = (
        P("seq", "head"),
        P("seq", "head"),
        P("seq", "head"),
        P("seq", "head"),
        P("seq", "head"),
    )
    return jax.shard_map(shards, mesh=mesh, in_specs=in_specs, out_specs=out_specs, check_vma=False)
```

```python
import functools

import jax
import jax.numpy as jnp
from jax import lax
from jax.experimental import pallas as pl
from jax.experimental.pallas import tpu as pltpu
from jax.sharding import PartitionSpec as P

MESH = pl.DeviceIdType.MESH
BF16 = jnp.bfloat16
F32 = jnp.float32
SPAN = 256
COLS = 384
HEAD_DIM = 64
LANES = 128
HALF = 128
PIECE = SPAN + HALF
SLOTS = 6
WINDOW = 5
X_SIZE = 4
Y_SIZE = 4
HEAD_SIZE = 4
NN = (((1,), (0,)), ((), ()))
NT = (((1,), (1,)), ((), ()))
K, Q, V, DO, ATT, DQ, DK, DV = range(8)


def product(left, right, dims):
    return lax.dot_general(left, right, dims, preferred_element_type=F32)


def low_lanes(rows):
    return lax.broadcasted_iota(jnp.int32, (rows, LANES), 1) < HEAD_DIM


def swap(block):
    return pltpu.roll(block, HEAD_DIM, 1)


def fold(block):
    return jnp.where(low_lanes(HALF), block[:HALF], swap(block[HALF:]))


def to_pieces(tiles, piece_ref, scale=None):
    first, middle, last = [tile.astype(F32) for tile in tiles]
    if scale is not None:
        first, middle, last = first * scale, middle * scale, last * scale
    swapped = swap(middle)
    piece_ref[0, :SPAN] = first.astype(BF16)
    piece_ref[0, SPAN:] = jnp.where(low_lanes(HALF), middle[:HALF], swapped[HALF:]).astype(BF16)
    piece_ref[1, :SPAN] = last.astype(BF16)
    piece_ref[1, SPAN:] = jnp.where(low_lanes(HALF), swapped[:HALF], middle[HALF:]).astype(BF16)


def from_pieces(piece_ref, out_ref):
    out_ref[:, 0:LANES] = piece_ref[0, :SPAN]
    out_ref[:, 2 * LANES : 3 * LANES] = piece_ref[1, :SPAN]
    low = piece_ref[0, SPAN:].astype(F32)
    high = piece_ref[1, SPAN:].astype(F32)
    top = jnp.where(low_lanes(HALF), low, swap(high))
    bottom = jnp.where(low_lanes(HALF), swap(low), high)
    out_ref[:HALF, LANES : 2 * LANES] = top.astype(BF16)
    out_ref[HALF:, LANES : 2 * LANES] = bottom.astype(BF16)


def unfold(third):
    wide = third.astype(F32)
    return jnp.concatenate([wide, swap(wide)], axis=0)


def layer_kernel(
    z_size,
    q_hbm, k_hbm, v_hbm, w_hbm, g_hbm,
    proj_out, dq_out, dk_out, dv_out, dw_out,
    proj_ref, dq_ref, dk_ref, dv_ref, dw_ref,
    q_ref, k_ref, v_ref, w_ref, packs, q_in, do_in, k_in, v_in, att_in, dq_in, dk_in, dv_in,
    grads, grads_t, k_nat, v_nat, k_tr, v_tr, q_tr, do_tr,
    scores, weights, inverse, att_tr, dq_tr, dk_acc, dv_acc,
    near_send, near_in, back_send, back_in, attended,
    proj_send, proj_in, proj_keep, hip_send, hip_in,
    x_terms, x_in, z_send, z_in, z_terms, z_first_in, x_send, x_last_in, y_send, y_in, sums,
    load_sems, store_sems, a2a_send_sems, a2a_recv_sems, flow_sems, near_sems, back_sems, term_sems,
    grad_send_sems, grad_recv_sems, proj_send_sems, proj_recv_sems, x_sems, z_sems, z_first_sems, x_last_sems, y_sems,
):
    seq = lax.axis_index("seq")
    head = lax.axis_index("head")
    rows = z_size * X_SIZE
    y_at = seq % Y_SIZE
    row_at = seq // Y_SIZE
    x_at = row_at % X_SIZE
    z_at = row_at // X_SIZE
    core = head % 2
    high = head // 2
    y_half = y_at // 2
    y_low = y_at % 2

    def at_row(row):
        return (row % rows) * Y_SIZE + y_at

    partners = [(row_at * Y_SIZE + 2 * core + j, 2 * high + y_half) for j in range(2)]
    is_self = [(y_half == core) & (y_low == j) for j in range(2)]
    other = 2 * high + 1 - core
    after = (at_row(row_at + 1), head)
    before = (at_row(row_at + rows - 1), head)
    sibling = (seq, other)
    across = (seq, 2 * (1 - high) + core)

    has_after = row_at < rows - 1
    has_before = row_at > 0

    def x_peer(step):
        return (x_at + step) % X_SIZE

    def z_peer(step):
        return (z_at + step) % z_size

    def y_peer(step):
        return (y_at + step) % Y_SIZE

    def device(z, x, y):
        return ((z * X_SIZE + x) * Y_SIZE + y, head)

    barrier = pltpu.get_barrier_semaphore()

    def greet(target):
        pl.semaphore_signal(barrier, inc=1, device_id=target, device_id_type=MESH)

    for j in range(2):
        pl.when(jnp.logical_not(is_self[j]))(functools.partial(greet, partners[j]))
    pl.when(has_after)(functools.partial(greet, after))
    pl.when(has_before)(functools.partial(greet, before))
    greet(sibling)
    greet(across)
    for step in range(1, X_SIZE):
        greet(device(z_at, x_peer(step), y_at))
    for step in range(1, z_size):
        greet(device(z_peer(step), x_at, y_at))
    for step in range(1, Y_SIZE):
        greet(device(z_at, x_at, y_peer(step)))

    def tiles_of(ref):
        return [ref[:, t * LANES : (t + 1) * LANES] for t in range(3)]

    loads = {}
    for at, (name, src, dst) in enumerate(
        (("k", k_hbm, k_ref), ("v", v_hbm, v_ref), ("q", q_hbm, q_ref), ("g", g_hbm, grads.at[head]), ("w", w_hbm, w_ref))
    ):
        loads[name] = pltpu.make_async_copy(src, dst, load_sems.at[at])
        loads[name].start()
    loads["k"].wait()
    to_pieces(tiles_of(k_ref), packs.at[K])
    loads["v"].wait()
    to_pieces(tiles_of(v_ref), packs.at[V])
    loads["q"].wait()
    to_pieces(tiles_of(q_ref), packs.at[Q], HEAD_DIM**-0.5)
    loads["g"].wait()

    @pl.when(jnp.logical_not(has_before))
    def _():
        k_in[0:2] = jnp.zeros((2, PIECE, LANES), BF16)
        v_in[0:2] = jnp.zeros((2, PIECE, LANES), BF16)

    @pl.when(jnp.logical_not(has_before) & (core == 0))
    def _():
        k_in[2:4] = jnp.zeros((2, PIECE, LANES), BF16)
        v_in[2:4] = jnp.zeros((2, PIECE, LANES), BF16)

    @pl.when(jnp.logical_not(has_after))
    def _():
        back_in[...] = jnp.zeros(back_in.shape, BF16)

    greeted = X_SIZE + Y_SIZE + z_size - 3 + 6 - jnp.where(y_half == core, 1, 0)
    greeted -= jnp.where(has_after, 0, 1) + jnp.where(has_before, 0, 1)
    pl.semaphore_wait(barrier, greeted)

    started = []
    stores = []

    def store(src, dst):
        copy = pltpu.make_async_copy(src, dst, store_sems.at[len(stores)])
        copy.start()
        stores.append(copy)


    def remote(src, dst, send_sem, recv_sem, target):
        return pltpu.make_async_remote_copy(
            src_ref=src, dst_ref=dst, send_sem=send_sem, recv_sem=recv_sem, device_id=target, device_id_type=MESH
        )

    def send(*args):
        copy = remote(*args)
        copy.start()
        started.append(copy)
        return copy

    waits = []

    def swap_start(kind, j, src, dst):
        copy = remote(src, dst, a2a_send_sems.at[kind, j], a2a_recv_sems.at[kind, y_low], partners[j])
        pl.when(jnp.logical_not(is_self[j]))(copy.start)
        pl.when(is_self[j])(pltpu.make_async_copy(src, dst, a2a_recv_sems.at[kind, y_low]).start)
        waits.append((jnp.logical_not(is_self[j]), copy.wait_send))

    def swap_wait(kind, j, dst):
        remote(dst, dst, a2a_send_sems.at[kind, j], a2a_recv_sems.at[kind, j], partners[j]).wait_recv()

    def grad_send(index, step, target):
        return send(grads.at[index], grads.at[index], grad_send_sems.at[step - 1], grad_recv_sems.at[step - 1], target)

    own = head
    own_across = 2 * (1 - high) + core
    from_step = {1: other, 2: own_across, 3: 2 * (1 - high) + 1 - core}

    def grad_wait(step):
        slot = grads.at[from_step[step]]
        remote(slot, slot, grad_send_sems.at[step - 1], grad_recv_sems.at[step - 1], across).wait_recv()

    for kind, buffer in ((K, k_in), (V, v_in)):
        for j in range(2):
            swap_start(kind, j, packs.at[kind, j], buffer.at[4 + y_low])
    for j in range(2):
        swap_start(Q, j, packs.at[Q, j], q_in.at[y_low])

    def near_copy(at, buffer, slot, j):
        return remote(
            buffer.at[slot + j], buffer.at[2 + j], near_sems.at[0, at, j], near_sems.at[1, at, j], sibling
        )

    def far_copy(at, buffer, j):
        return remote(buffer.at[4 + j], buffer.at[j], flow_sems.at[0, at, j], flow_sems.at[1, at, j], after)

    def flow(at, kind, buffer):
        for j in range(2):
            swap_wait(kind, j, buffer.at[4 + j])
            far = far_copy(at, buffer, j)
            pl.when(has_after)(far.start)
            waits.append((has_after, far.wait_send))
            near = near_copy(at, buffer, 4, j)
            pl.when(core == 0)(near.start)
            waits.append(((core == 0) | has_before, near.wait_send))

    def flow_on(at, buffer):
        for j in range(2):
            pl.when(has_before)(
                remote(buffer.at[j], buffer.at[j], flow_sems.at[0, at, j], flow_sems.at[1, at, j], before).wait_recv
            )
            pl.when((core == 1) & has_before)(near_copy(at, buffer, 0, j).start)

    def near_wait(at, buffer):
        for j in range(2):
            pl.when((core == 1) | has_before)(near_copy(at, buffer, 2, j).wait_recv)

    def spread(buffer, natural, turned, slot):
        first = buffer[slot, :SPAN]
        third = unfold(buffer[slot, SPAN:])
        natural[0, slot] = first
        natural[1, slot] = third.astype(BF16)
        turned[0, slot] = first.astype(F32).T.astype(BF16)
        turned[1, slot] = third.T.astype(BF16)

    def turn(buffer, turned, j):
        first = buffer[j, :SPAN].astype(F32).T
        third = unfold(buffer[j, SPAN:]).T
        upper = lax.broadcasted_iota(jnp.int32, (LANES, SPAN), 0) < HEAD_DIM
        turned[3 * j] = jnp.where(upper, first, 0.0).astype(BF16)
        turned[3 * j + 1] = jnp.where(upper, 0.0, first).astype(BF16)
        turned[3 * j + 2] = jnp.where(upper, third, 0.0).astype(BF16)

    flow(0, K, k_in)
    flow(1, V, v_in)
    grad_send(own, 2, across)
    grad_send(own, 1, sibling)
    for slot in (4, 5):
        spread(k_in, k_nat, k_tr, slot)
        spread(v_in, v_nat, v_tr, slot)
    for j in range(2):
        swap_wait(Q, j, q_in.at[j])
        turn(q_in, q_tr, j)
    flow_on(0, k_in)
    for slot in (0, 1):
        spread(k_in, k_nat, k_tr, slot)
    flow_on(1, v_in)
    near_wait(0, k_in)
    for slot in (2, 3):
        spread(k_in, k_nat, k_tr, slot)
    for slot in (0, 1):
        spread(v_in, v_nat, v_tr, slot)
    near_wait(1, v_in)
    for slot in (2, 3):
        spread(v_in, v_nat, v_tr, slot)

    def seen(slot):
        return (row_at > 0) | (slot >= 4 - 2 * core)

    def place(i, h):
        return h // 2, pl.multiple_of((h % 2) * HEAD_DIM, HEAD_DIM), 3 * i + h

    def forward_unit(i, h):
        tile, first, unit = place(i, h)
        query = q_tr[unit]
        top = None
        for j in range(WINDOW):
            block = product(k_nat[tile, i + j], query, NN)
            block = jnp.where(seen(i + j), block, -1e30)
            scores[j] = block
            peak = jnp.max(block, axis=0, keepdims=True)
            top = peak if top is None else jnp.maximum(top, peak)
        total = jnp.zeros((1, SPAN), F32)
        acc = jnp.zeros((HEAD_DIM, SPAN), F32)
        for j in range(WINDOW):
            part = jnp.exp(scores[j] - top)
            total += jnp.sum(part, axis=0, keepdims=True)
            part = part.astype(BF16)
            weights[unit, j] = part
            acc += product(v_tr[tile, i + j, pl.ds(first, HEAD_DIM), :], part, NN)
        share = 1.0 / total
        inverse[unit] = share
        att_tr[i, tile, pl.ds(first, HEAD_DIM), :] = acc * share

    def pack_turned(turned, kind, i):
        packs[kind, i, :SPAN] = turned[i, 0].T.astype(BF16)
        packs[kind, i, SPAN:] = fold(turned[i, 1].T).astype(BF16)

    for i in range(2):
        att_tr[i, 1] = jnp.zeros((LANES, SPAN), F32)
        dq_tr[i, 1] = jnp.zeros((LANES, SPAN), F32)
    dk_acc[...] = jnp.zeros(dk_acc.shape, F32)
    dv_acc[...] = jnp.zeros(dv_acc.shape, F32)

    def forward(i):
        pl.loop(0, 3)(functools.partial(forward_unit, i))
        pack_turned(att_tr, ATT, i)
        swap_start(ATT, i, packs.at[ATT, i], att_in.at[y_low])

    forward(0)
    grad_wait(2)
    grad_send(own_across, 3, sibling)
    forward(1)
    loads["w"].wait()
    grad_wait(1)
    grad_wait(3)
    acc = product(grads[0], w_ref[0:COLS], NN)
    for index in range(1, HEAD_SIZE):
        acc += product(grads[index], w_ref[index * COLS : (index + 1) * COLS], NN)
    to_pieces([acc[:, t * LANES : (t + 1) * LANES] for t in range(3)], packs.at[DO])
    for j in range(2):
        swap_start(DO, j, packs.at[DO, j], do_in.at[y_low])
    for index in range(HEAD_SIZE):
        grads_t[index] = grads[index].astype(F32).T.astype(BF16)

    def backward_unit(i, h):
        tile, first, unit = place(i, h)
        query = q_tr[unit]
        d_out = (do_tr[unit].astype(F32) * inverse[unit]).astype(BF16)
        do_tr[unit] = d_out
        d_half = do_tr[unit, pl.ds(first, HEAD_DIM), :].astype(F32)
        att_half = att_tr[i, tile, pl.ds(first, HEAD_DIM), :].astype(BF16).astype(F32)
        delta = jnp.sum(d_half * att_half, axis=0, keepdims=True)
        acc = jnp.zeros((HEAD_DIM, SPAN), F32)
        for j in range(WINDOW):
            part = weights[unit, j]
            d_part = product(v_nat[tile, i + j], d_out, NN)
            d_score = (part.astype(F32) * (d_part - delta)).astype(BF16)
            dk_acc[tile, i + j] += product(d_score, query, NT)
            dv_acc[tile, i + j] += product(part, d_out, NT)
            acc += product(k_tr[tile, i + j, pl.ds(first, HEAD_DIM), :], d_score, NN)
        dq_tr[i, tile, pl.ds(first, HEAD_DIM), :] = acc * (HEAD_DIM**-0.5)

    for j in range(2):
        swap_wait(ATT, j, att_in.at[j])
    from_pieces(att_in, attended)
    att = attended[...]

    def projection(index):
        weight = w_ref[pl.ds(pl.multiple_of(index * COLS, COLS), COLS), :]
        return product(att, weight, NT)

    block = x_terms.shape[2]
    x_cols = x_terms.shape[3]
    per_z = X_SIZE * block
    for index in range(HEAD_SIZE):
        term = product(grads_t[index], att, NN).astype(BF16)
        for part in range(COLS // per_z):
            for x in range(X_SIZE):
                start = part * per_z + x * block
                z = index * (COLS // per_z) + part
                x_terms[z, x] = term[start : start + block, :x_cols]
                z_terms[z, x] = term[start : start + block, x_cols:]
    x_copies = []
    for step in range(1, X_SIZE):
        x_copies.append(
            send(
                x_terms.at[:, x_peer(step)],
                x_in.at[step - 1],
                x_sems.at[0, step - 1],
                x_sems.at[1, step - 1],
                device(z_at, x_peer(step), y_at),
            )
        )
    z_first_copies = []
    for step in range(1, z_size):
        z_first_copies.append(
            send(
                z_terms.at[z_peer(step)],
                z_first_in.at[step - 1],
                z_first_sems.at[0, step - 1],
                z_first_sems.at[1, step - 1],
                device(z_peer(step), x_at, y_at),
            )
        )
    for at, index in enumerate((2 * (1 - high) + 1 - core, 2 * high + 1 - core)):
        proj_send[at] = projection(index).astype(BF16)
        send(proj_send.at[at], proj_in.at[at], proj_send_sems.at[at], proj_recv_sems.at[at], sibling)
    proj_keep[0] = projection(own_across)
    proj_keep[1] = projection(own)

    for j in range(2):
        swap_wait(DO, j, do_in.at[j])
        turn(do_in, do_tr, j)
    for i in range(2):
        pl.loop(0, 3)(functools.partial(backward_unit, i))
        pack_turned(dq_tr, DQ, i)
        swap_start(DQ, i, packs.at[DQ, i], dq_in.at[y_low])
        if i == 0:
            remote(proj_send.at[0], proj_in.at[0], proj_send_sems.at[0], proj_recv_sems.at[0], sibling).wait_recv()
            hip_send[...] = (proj_keep[0] + proj_in[0].astype(F32)).astype(BF16)
            hip_copy = send(hip_send, hip_in, proj_send_sems.at[2], proj_recv_sems.at[2], across)

    accs = (dk_acc, dv_acc)

    def term_copy(at, j):
        return remote(
            near_send.at[at, j], near_in.at[at, j], term_sems.at[0, at, j], term_sems.at[1, at, j], sibling
        )

    def back_copy(at, j, target):
        return remote(
            back_send.at[at, j], back_in.at[at, j], back_sems.at[0, at, j], back_sems.at[1, at, j], target
        )

    def send_back(summed):
        for at in range(2):
            for j in range(2):
                tile = accs[at][0, j]
                third = fold(accs[at][1, j])
                if summed:
                    term_copy(at, j).wait_recv()
                    tile += near_in[at, j, :SPAN].astype(F32)
                    third += near_in[at, j, SPAN:].astype(F32)
                back_send[at, j, :SPAN] = tile.astype(BF16)
                back_send[at, j, SPAN:] = third.astype(BF16)
                pl.when(has_before)(back_copy(at, j, before).start)

    for at in range(2):
        for j in range(2):
            near_send[at, j, :SPAN] = accs[at][0, 2 + j].astype(BF16)
            near_send[at, j, SPAN:] = fold(accs[at][1, 2 + j]).astype(BF16)
            copy = term_copy(at, j)
            copy.start()
            started.append(copy)
            waits.append((has_before, back_copy(at, j, before).wait_send))
    pl.when(core == 0)(functools.partial(send_back, False))
    pl.when(core == 1)(functools.partial(send_back, True))

    for copy in x_copies:
        copy.wait_recv()
    for z in range(z_size):
        total = x_terms[z, x_at].astype(F32)
        for step in range(1, X_SIZE):
            total += x_in[step - 1, z].astype(F32)
        z_send[z] = total.astype(BF16)
    z_copies = []
    for step in range(1, z_size):
        z_copies.append(
            send(
                z_send.at[z_peer(step)],
                z_in.at[step - 1],
                z_sems.at[0, step - 1],
                z_sems.at[1, step - 1],
                device(z_peer(step), x_at, y_at),
            )
        )
    for copy in z_first_copies:
        copy.wait_recv()
    for x in range(X_SIZE):
        total = z_terms[z_at, x].astype(F32)
        for step in range(1, z_size):
            total += z_first_in[step - 1, x].astype(F32)
        x_send[x] = total.astype(BF16)
    x_last_copies = []
    for step in range(1, X_SIZE):
        x_last_copies.append(
            send(
                x_send.at[x_peer(step)],
                x_last_in.at[step - 1],
                x_last_sems.at[0, step - 1],
                x_last_sems.at[1, step - 1],
                device(z_at, x_peer(step), y_at),
            )
        )

    def finish(near):
        for at in range(2):
            for j in range(2):
                tile = accs[at][0, 4 + j]
                third = fold(accs[at][1, 4 + j])
                if near:
                    term_copy(at, j).wait_recv()
                    tile += near_in[at, j, :SPAN].astype(F32)
                    third += near_in[at, j, SPAN:].astype(F32)
                pl.when(has_after)(back_copy(at, j, after).wait_recv)
                tile += back_in[at, j, :SPAN].astype(F32)
                third += back_in[at, j, SPAN:].astype(F32)
                kind = (DK, DV)[at]
                packs[kind, j, :SPAN] = tile.astype(BF16)
                packs[kind, j, SPAN:] = third.astype(BF16)
                swap_start(kind, j, packs.at[kind, j], (dk_in, dv_in)[at].at[y_low])

    finish_waits = len(waits)
    pl.when(core == 0)(functools.partial(finish, True))
    del waits[finish_waits:]
    pl.when(core == 1)(functools.partial(finish, False))
    del waits[finish_waits:]
    for kind, buffer in ((DK, dk_in), (DV, dv_in)):
        for j in range(2):
            src = packs.at[kind, j]
            copy = remote(src, src, a2a_send_sems.at[kind, j], a2a_recv_sems.at[kind, y_low], partners[j])
            waits.append((jnp.logical_not(is_self[j]), copy.wait_send))

    for copy in z_copies:
        copy.wait_recv()
    sums[:, :x_cols] = z_send[z_at].astype(F32)
    for step in range(1, z_size):
        sums[:, :x_cols] += z_in[step - 1].astype(F32)
    for copy in x_last_copies:
        copy.wait_recv()
    sums[:, x_cols:] = x_send[x_at].astype(F32)
    for step in range(1, X_SIZE):
        sums[:, x_cols:] += x_last_in[step - 1].astype(F32)
    out_rows = dw_ref.shape[0]
    for piece in range(Y_SIZE):
        y_send[piece, 0:out_rows] = sums[piece * out_rows : (piece + 1) * out_rows]
    y_copies = []
    for step in range(1, Y_SIZE):
        y_copies.append(
            send(
                y_send.at[y_peer(step)],
                y_in.at[step - 1],
                y_sems.at[0, step - 1],
                y_sems.at[1, step - 1],
                device(z_at, x_at, y_peer(step)),
            )
        )

    for j in range(2):
        swap_wait(DQ, j, dq_in.at[j])
    from_pieces(dq_in, dq_ref)
    store(dq_ref, dq_out)
    remote(proj_send.at[1], proj_in.at[1], proj_send_sems.at[1], proj_recv_sems.at[1], sibling).wait_recv()
    hip_copy.wait_recv()
    proj_ref[...] = (proj_keep[1] + proj_in[1].astype(F32) + hip_in[...].astype(F32)).astype(BF16)
    store(proj_ref, proj_out)
    for j in range(2):
        swap_wait(DK, j, dk_in.at[j])
    from_pieces(dk_in, dk_ref)
    store(dk_ref, dk_out)
    for j in range(2):
        swap_wait(DV, j, dv_in.at[j])
    from_pieces(dv_in, dv_ref)
    store(dv_ref, dv_out)
    result = y_send[y_at]
    for step in range(1, Y_SIZE):
        y_copies[step - 1].wait_recv()
        result += y_in[step - 1]
    dw_ref[...] = result[0:out_rows]
    store(dw_ref, dw_out)

    for copy in started:
        copy.wait_send()
    for sent, wait in waits:
        pl.when(sent)(wait)
    for copy in stores:
        copy.wait()


def results_kernel(*refs):
    sems = refs[-1]
    count = (len(refs) - 1) // 3
    sources, targets, held = refs[:count], refs[count : 2 * count], refs[2 * count : 3 * count]
    loads = [pltpu.make_async_copy(sources[at], held[at], sems.at[0, at]) for at in range(count)]
    stores = [pltpu.make_async_copy(held[at], targets[at], sems.at[1, at]) for at in range(count)]
    for copy in loads:
        copy.start()
    for load, copy in zip(loads, stores):
        load.wait()
        copy.start()
    for copy in stores:
        copy.wait()


def shards(query_rows, key_rows, value_rows, out_weight, out_grad):
    seq_size = lax.axis_size("seq")
    z_size = seq_size // (X_SIZE * Y_SIZE)
    out_rows = out_weight.shape[0] // seq_size
    block = out_rows * Y_SIZE
    padded = (out_rows + 7) // 8 * 8
    x_cols = 2 * LANES
    rows_out = jax.ShapeDtypeStruct((SPAN, COLS), BF16)
    vmem = pltpu.VMEM
    dma = pltpu.SemaphoreType.DMA
    piece = (PIECE, LANES)
    scratch = [
        vmem((SPAN, COLS), BF16),
        vmem((SPAN, COLS), BF16),
        vmem((SPAN, COLS), BF16),
        vmem((SPAN, COLS), BF16),
        vmem((out_rows, COLS), F32),
        vmem((SPAN, COLS), BF16),
        vmem((SPAN, COLS), BF16),
        vmem((SPAN, COLS), BF16),
        vmem(out_weight.shape, BF16),
        vmem((8, 2) + piece, BF16),
        vmem((2,) + piece, BF16),
        vmem((2,) + piece, BF16),
        vmem((SLOTS,) + piece, BF16),
        vmem((SLOTS,) + piece, BF16),
        vmem((2,) + piece, BF16),
        vmem((2,) + piece, BF16),
        vmem((2,) + piece, BF16),
        vmem((2,) + piece, BF16),
        vmem((HEAD_SIZE, SPAN, COLS), BF16),
        vmem((HEAD_SIZE, COLS, SPAN), BF16),
        vmem((2, SLOTS, SPAN, LANES), BF16),
        vmem((2, SLOTS, SPAN, LANES), BF16),
        vmem((2, SLOTS, LANES, SPAN), BF16),
        vmem((2, SLOTS, LANES, SPAN), BF16),
        vmem((6, LANES, SPAN), BF16),
        vmem((6, LANES, SPAN), BF16),
        vmem((WINDOW, SPAN, SPAN), F32),
        vmem((6, WINDOW, SPAN, SPAN), BF16),
        vmem((6, 1, SPAN), F32),
        vmem((2, 2, LANES, SPAN), F32),
        vmem((2, 2, LANES, SPAN), F32),
        vmem((2, SLOTS, SPAN, LANES), F32),
        vmem((2, SLOTS, SPAN, LANES), F32),
        vmem((2, 2) + piece, BF16),
        vmem((2, 2) + piece, BF16),
        vmem((2, 2) + piece, BF16),
        vmem((2, 2) + piece, BF16),
        vmem((SPAN, COLS), BF16),
        vmem((2, SPAN, COLS), BF16),
        vmem((2, SPAN, COLS), BF16),
        vmem((2, SPAN, COLS), F32),
        vmem((SPAN, COLS), BF16),
        vmem((SPAN, COLS), BF16),
        vmem((z_size, X_SIZE, block, x_cols), BF16),
        vmem((X_SIZE - 1, z_size, block, x_cols), BF16),
        vmem((z_size, block, x_cols), BF16),
        vmem((z_size - 1, block, x_cols), BF16),
        vmem((z_size, X_SIZE, block, COLS - x_cols), BF16),
        vmem((z_size - 1, X_SIZE, block, COLS - x_cols), BF16),
        vmem((X_SIZE, block, COLS - x_cols), BF16),
        vmem((X_SIZE - 1, block, COLS - x_cols), BF16),
        vmem((Y_SIZE, padded, COLS), F32),
        vmem((Y_SIZE - 1, padded, COLS), F32),
        vmem((block, COLS), F32),
        dma((5,)),
        dma((5,)),
        dma((8, 2)),
        dma((8, 2)),
        dma((2, 2, 2)),
        dma((2, 2, 2)),
        dma((2, 2, 2)),
        dma((2, 2, 2)),
        dma((3,)),
        dma((3,)),
        dma((3,)),
        dma((3,)),
        dma((2, X_SIZE - 1)),
        dma((2, z_size - 1)),
        dma((2, z_size - 1)),
        dma((2, X_SIZE - 1)),
        dma((2, Y_SIZE - 1)),
    ]
    outputs = (rows_out,) * 4 + (jax.ShapeDtypeStruct((out_rows, COLS), F32),)
    anywhere = pl.BlockSpec(memory_space=pl.ANY)
    results = pl.pallas_call(
        functools.partial(layer_kernel, z_size),
        out_shape=outputs,
        in_specs=[anywhere] * 5,
        out_specs=(anywhere,) * 5,
        scratch_shapes=scratch,
        compiler_params=pltpu.CompilerParams(
            collective_id=0, has_side_effects=True, vmem_limit_bytes=60 * 1024 * 1024
        ),
    )(query_rows, key_rows, value_rows, out_weight, out_grad)
    return pl.pallas_call(
        results_kernel,
        out_shape=outputs,
        in_specs=[anywhere] * 5,
        out_specs=(anywhere,) * 5,
        scratch_shapes=[vmem(kept.shape, kept.dtype) for kept in outputs] + [dma((2, 5))],
        compiler_params=pltpu.CompilerParams(vmem_limit_bytes=60 * 1024 * 1024),
    )(*results)


def solution(mesh):
    in_specs = (
        P("seq", "head"),
        P("seq", "head"),
        P("seq", "head"),
        P(None, "head"),
        P("seq", "head"),
    )
    out_specs = (
        P("seq", "head"),
        P("seq", "head"),
        P("seq", "head"),
        P("seq", "head"),
        P("seq", "head"),
    )
    return jax.shard_map(shards, mesh=mesh, in_specs=in_specs, out_specs=out_specs, check_vma=False)
```

```python
import functools

import jax
import jax.numpy as jnp
from jax import lax
from jax.experimental import pallas as pl
from jax.experimental.pallas import tpu as pltpu
from jax.sharding import PartitionSpec as P

MESH = pl.DeviceIdType.MESH
BF16 = jnp.bfloat16
F32 = jnp.float32
SPAN = 256
COLS = 384
HEAD_DIM = 64
LANES = 128
HALF = 128
PIECE = SPAN + HALF
SLOTS = 6
WINDOW = 5
X_SIZE = 4
Y_SIZE = 4
HEAD_SIZE = 4
NN = (((1,), (0,)), ((), ()))
NT = (((1,), (1,)), ((), ()))
K, Q, V, DO, ATT, DQ, DK, DV = range(8)


def product(left, right, dims):
    return lax.dot_general(left, right, dims, preferred_element_type=F32)


def low_lanes(rows):
    return lax.broadcasted_iota(jnp.int32, (rows, LANES), 1) < HEAD_DIM


def swap(block):
    return pltpu.roll(block, HEAD_DIM, 1)


def fold(block):
    return jnp.where(low_lanes(HALF), block[:HALF], swap(block[HALF:]))


def to_pieces(tiles, piece_ref, scale=None):
    first, middle, last = [tile.astype(F32) for tile in tiles]
    if scale is not None:
        first, middle, last = first * scale, middle * scale, last * scale
    swapped = swap(middle)
    piece_ref[0, :SPAN] = first.astype(BF16)
    piece_ref[0, SPAN:] = jnp.where(low_lanes(HALF), middle[:HALF], swapped[HALF:]).astype(BF16)
    piece_ref[1, :SPAN] = last.astype(BF16)
    piece_ref[1, SPAN:] = jnp.where(low_lanes(HALF), swapped[:HALF], middle[HALF:]).astype(BF16)


def from_pieces(piece_ref, out_ref):
    out_ref[:, 0:LANES] = piece_ref[0, :SPAN]
    out_ref[:, 2 * LANES : 3 * LANES] = piece_ref[1, :SPAN]
    low = piece_ref[0, SPAN:].astype(F32)
    high = piece_ref[1, SPAN:].astype(F32)
    top = jnp.where(low_lanes(HALF), low, swap(high))
    bottom = jnp.where(low_lanes(HALF), swap(low), high)
    out_ref[:HALF, LANES : 2 * LANES] = top.astype(BF16)
    out_ref[HALF:, LANES : 2 * LANES] = bottom.astype(BF16)


def unfold(third):
    wide = third.astype(F32)
    return jnp.concatenate([wide, swap(wide)], axis=0)


def layer_kernel(
    z_size,
    q_hbm, k_hbm, v_hbm, w_hbm, g_hbm,
    proj_out, dq_out, dk_out, dv_out, dw_out,
    proj_ref, dq_ref, dk_ref, dv_ref, dw_ref,
    q_ref, k_ref, v_ref, w_ref, packs, q_in, do_in, k_in, v_in, att_in, dq_in, dk_in, dv_in,
    grads, grads_t, k_nat, v_nat, k_tr, v_tr, q_tr, do_tr,
    scores, weights, inverse, att_tr, dq_tr, dk_acc, dv_acc,
    near_send, near_in, back_send, back_in, attended,
    proj_send, proj_in, proj_keep, hip_send, hip_in,
    x_terms, x_in, z_send, z_in, z_terms, z_first_in, x_send, x_last_in, y_send, y_in, sums,
    load_sems, store_sems, a2a_send_sems, a2a_recv_sems, flow_sems, near_sems, back_sems, term_sems,
    grad_send_sems, grad_recv_sems, proj_send_sems, proj_recv_sems, x_sems, z_sems, z_first_sems, x_last_sems, y_sems,
):
    seq = lax.axis_index("seq")
    head = lax.axis_index("head")
    rows = z_size * X_SIZE
    y_at = seq % Y_SIZE
    row_at = seq // Y_SIZE
    x_at = row_at % X_SIZE
    z_at = row_at // X_SIZE
    core = head % 2
    high = head // 2
    y_half = y_at // 2
    y_low = y_at % 2

    def at_row(row):
        return (row % rows) * Y_SIZE + y_at

    partners = [(row_at * Y_SIZE + 2 * core + j, 2 * high + y_half) for j in range(2)]
    is_self = [(y_half == core) & (y_low == j) for j in range(2)]
    other = 2 * high + 1 - core
    after = (at_row(row_at + 1), head)
    before = (at_row(row_at + rows - 1), head)
    sibling = (seq, other)
    across = (seq, 2 * (1 - high) + core)

    has_after = row_at < rows - 1
    has_before = row_at > 0

    def x_peer(step):
        return (x_at + step) % X_SIZE

    def z_peer(step):
        return (z_at + step) % z_size

    def y_peer(step):
        return (y_at + step) % Y_SIZE

    def device(z, x, y):
        return ((z * X_SIZE + x) * Y_SIZE + y, head)

    barrier = pltpu.get_barrier_semaphore()

    def greet(target):
        pl.semaphore_signal(barrier, inc=1, device_id=target, device_id_type=MESH)

    for j in range(2):
        pl.when(jnp.logical_not(is_self[j]))(functools.partial(greet, partners[j]))
    pl.when(has_after)(functools.partial(greet, after))
    pl.when(has_before)(functools.partial(greet, before))
    greet(sibling)
    greet(across)
    for step in range(1, X_SIZE):
        greet(device(z_at, x_peer(step), y_at))
    for step in range(1, z_size):
        greet(device(z_peer(step), x_at, y_at))
    for step in range(1, Y_SIZE):
        greet(device(z_at, x_at, y_peer(step)))

    def tiles_of(ref):
        return [ref[:, t * LANES : (t + 1) * LANES] for t in range(3)]

    loads = {}
    for at, (name, src, dst) in enumerate(
        (("k", k_hbm, k_ref), ("v", v_hbm, v_ref), ("q", q_hbm, q_ref), ("g", g_hbm, grads.at[head]), ("w", w_hbm, w_ref))
    ):
        loads[name] = pltpu.make_async_copy(src, dst, load_sems.at[at])
        loads[name].start()
    loads["k"].wait()
    to_pieces(tiles_of(k_ref), packs.at[K])
    loads["v"].wait()
    to_pieces(tiles_of(v_ref), packs.at[V])
    loads["q"].wait()
    to_pieces(tiles_of(q_ref), packs.at[Q], HEAD_DIM**-0.5)
    loads["g"].wait()

    @pl.when(jnp.logical_not(has_before))
    def _():
        k_in[0:2] = jnp.zeros((2, PIECE, LANES), BF16)
        v_in[0:2] = jnp.zeros((2, PIECE, LANES), BF16)

    @pl.when(jnp.logical_not(has_before) & (core == 0))
    def _():
        k_in[2:4] = jnp.zeros((2, PIECE, LANES), BF16)
        v_in[2:4] = jnp.zeros((2, PIECE, LANES), BF16)

    @pl.when(jnp.logical_not(has_after))
    def _():
        back_in[...] = jnp.zeros(back_in.shape, BF16)

    greeted = X_SIZE + Y_SIZE + z_size - 3 + 6 - jnp.where(y_half == core, 1, 0)
    greeted -= jnp.where(has_after, 0, 1) + jnp.where(has_before, 0, 1)
    pl.semaphore_wait(barrier, greeted)

    started = []
    stores = []

    def store(src, dst):
        copy = pltpu.make_async_copy(src, dst, store_sems.at[len(stores)])
        copy.start()
        stores.append(copy)


    def remote(src, dst, send_sem, recv_sem, target):
        return pltpu.make_async_remote_copy(
            src_ref=src, dst_ref=dst, send_sem=send_sem, recv_sem=recv_sem, device_id=target, device_id_type=MESH
        )

    def send(*args):
        copy = remote(*args)
        copy.start()
        started.append(copy)
        return copy

    waits = []

    def swap_start(kind, j, src, dst):
        copy = remote(src, dst, a2a_send_sems.at[kind, j], a2a_recv_sems.at[kind, y_low], partners[j])
        pl.when(jnp.logical_not(is_self[j]))(copy.start)
        pl.when(is_self[j])(pltpu.make_async_copy(src, dst, a2a_recv_sems.at[kind, y_low]).start)
        waits.append((jnp.logical_not(is_self[j]), copy.wait_send))

    def swap_wait(kind, j, dst):
        remote(dst, dst, a2a_send_sems.at[kind, j], a2a_recv_sems.at[kind, j], partners[j]).wait_recv()

    def grad_send(index, step, target):
        return send(grads.at[index], grads.at[index], grad_send_sems.at[step - 1], grad_recv_sems.at[step - 1], target)

    own = head
    own_across = 2 * (1 - high) + core
    from_step = {1: other, 2: own_across, 3: 2 * (1 - high) + 1 - core}

    def grad_wait(step):
        slot = grads.at[from_step[step]]
        remote(slot, slot, grad_send_sems.at[step - 1], grad_recv_sems.at[step - 1], across).wait_recv()

    for kind, buffer in ((K, k_in), (V, v_in)):
        for j in range(2):
            swap_start(kind, j, packs.at[kind, j], buffer.at[4 + y_low])
    for j in range(2):
        swap_start(Q, j, packs.at[Q, j], q_in.at[y_low])

    def near_copy(at, buffer, slot, j):
        return remote(
            buffer.at[slot + j], buffer.at[2 + j], near_sems.at[0, at, j], near_sems.at[1, at, j], sibling
        )

    def far_copy(at, buffer, j):
        return remote(buffer.at[4 + j], buffer.at[j], flow_sems.at[0, at, j], flow_sems.at[1, at, j], after)

    def flow(at, kind, buffer):
        for j in range(2):
            swap_wait(kind, j, buffer.at[4 + j])
            far = far_copy(at, buffer, j)
            pl.when(has_after)(far.start)
            waits.append((has_after, far.wait_send))
            near = near_copy(at, buffer, 4, j)
            pl.when(core == 0)(near.start)
            waits.append(((core == 0) | has_before, near.wait_send))

    def flow_on(at, buffer):
        for j in range(2):
            pl.when(has_before)(
                remote(buffer.at[j], buffer.at[j], flow_sems.at[0, at, j], flow_sems.at[1, at, j], before).wait_recv
            )
            pl.when((core == 1) & has_before)(near_copy(at, buffer, 0, j).start)

    def near_wait(at, buffer):
        for j in range(2):
            pl.when((core == 1) | has_before)(near_copy(at, buffer, 2, j).wait_recv)

    def spread(buffer, natural, turned, slot):
        first = buffer[slot, :SPAN]
        third = unfold(buffer[slot, SPAN:])
        natural[0, slot] = first
        natural[1, slot] = third.astype(BF16)
        turned[0, slot] = first.astype(F32).T.astype(BF16)
        turned[1, slot] = third.T.astype(BF16)

    def turn(buffer, turned, j):
        first = buffer[j, :SPAN].astype(F32).T
        third = unfold(buffer[j, SPAN:]).T
        upper = lax.broadcasted_iota(jnp.int32, (LANES, SPAN), 0) < HEAD_DIM
        turned[3 * j] = jnp.where(upper, first, 0.0).astype(BF16)
        turned[3 * j + 1] = jnp.where(upper, 0.0, first).astype(BF16)
        turned[3 * j + 2] = jnp.where(upper, third, 0.0).astype(BF16)

    flow(0, K, k_in)
    flow(1, V, v_in)
    grad_send(own, 2, across)
    grad_send(own, 1, sibling)
    for slot in (4, 5):
        spread(k_in, k_nat, k_tr, slot)
        spread(v_in, v_nat, v_tr, slot)
    for j in range(2):
        swap_wait(Q, j, q_in.at[j])
        turn(q_in, q_tr, j)
    flow_on(0, k_in)
    for slot in (0, 1):
        spread(k_in, k_nat, k_tr, slot)
    flow_on(1, v_in)
    near_wait(0, k_in)
    for slot in (2, 3):
        spread(k_in, k_nat, k_tr, slot)
    for slot in (0, 1):
        spread(v_in, v_nat, v_tr, slot)
    near_wait(1, v_in)
    for slot in (2, 3):
        spread(v_in, v_nat, v_tr, slot)

    def seen(slot):
        return (row_at > 0) | (slot >= 4 - 2 * core)

    def place(i, h):
        return h // 2, pl.multiple_of((h % 2) * HEAD_DIM, HEAD_DIM), 3 * i + h

    def forward_unit(i, h):
        tile, first, unit = place(i, h)
        query = q_tr[unit]
        top = None
        for j in range(WINDOW):
            block = product(k_nat[tile, i + j], query, NN)
            block = jnp.where(seen(i + j), block, -1e30)
            scores[j] = block
            peak = jnp.max(block, axis=0, keepdims=True)
            top = peak if top is None else jnp.maximum(top, peak)
        total = jnp.zeros((1, SPAN), F32)
        acc = jnp.zeros((HEAD_DIM, SPAN), F32)
        for j in range(WINDOW):
            part = jnp.exp(scores[j] - top)
            total += jnp.sum(part, axis=0, keepdims=True)
            part = part.astype(BF16)
            weights[unit, j] = part
            acc += product(v_tr[tile, i + j, pl.ds(first, HEAD_DIM), :], part, NN)
        share = 1.0 / total
        inverse[unit] = share
        att_tr[i, tile, pl.ds(first, HEAD_DIM), :] = acc * share

    def pack_turned(turned, kind, i):
        packs[kind, i, :SPAN] = turned[i, 0].T.astype(BF16)
        packs[kind, i, SPAN:] = fold(turned[i, 1].T).astype(BF16)

    for i in range(2):
        att_tr[i, 1] = jnp.zeros((LANES, SPAN), F32)
        dq_tr[i, 1] = jnp.zeros((LANES, SPAN), F32)
    dk_acc[...] = jnp.zeros(dk_acc.shape, F32)
    dv_acc[...] = jnp.zeros(dv_acc.shape, F32)

    def forward(i):
        pl.loop(0, 3)(functools.partial(forward_unit, i))
        pack_turned(att_tr, ATT, i)
        swap_start(ATT, i, packs.at[ATT, i], att_in.at[y_low])

    forward(0)
    grad_wait(2)
    grad_send(own_across, 3, sibling)
    forward(1)
    loads["w"].wait()
    grad_wait(1)
    grad_wait(3)
    acc = product(grads[0], w_ref[0:COLS], NN)
    for index in range(1, HEAD_SIZE):
        acc += product(grads[index], w_ref[index * COLS : (index + 1) * COLS], NN)
    to_pieces([acc[:, t * LANES : (t + 1) * LANES] for t in range(3)], packs.at[DO])
    for j in range(2):
        swap_start(DO, j, packs.at[DO, j], do_in.at[y_low])
    for index in range(HEAD_SIZE):
        grads_t[index] = grads[index].astype(F32).T.astype(BF16)

    def backward_unit(i, h):
        tile, first, unit = place(i, h)
        query = q_tr[unit]
        d_out = (do_tr[unit].astype(F32) * inverse[unit]).astype(BF16)
        do_tr[unit] = d_out
        d_half = do_tr[unit, pl.ds(first, HEAD_DIM), :].astype(F32)
        att_half = att_tr[i, tile, pl.ds(first, HEAD_DIM), :].astype(BF16).astype(F32)
        delta = jnp.sum(d_half * att_half, axis=0, keepdims=True)
        acc = jnp.zeros((HEAD_DIM, SPAN), F32)
        for j in range(WINDOW):
            part = weights[unit, j]
            d_part = product(v_nat[tile, i + j], d_out, NN)
            d_score = (part.astype(F32) * (d_part - delta)).astype(BF16)
            dk_acc[tile, i + j] += product(d_score, query, NT)
            dv_acc[tile, i + j] += product(part, d_out, NT)
            acc += product(k_tr[tile, i + j, pl.ds(first, HEAD_DIM), :], d_score, NN)
        dq_tr[i, tile, pl.ds(first, HEAD_DIM), :] = acc * (HEAD_DIM**-0.5)

    for j in range(2):
        swap_wait(ATT, j, att_in.at[j])
    from_pieces(att_in, attended)
    att = attended[...]

    def projection(index):
        weight = w_ref[pl.ds(pl.multiple_of(index * COLS, COLS), COLS), :]
        return product(att, weight, NT)

    block = x_terms.shape[2]
    x_cols = x_terms.shape[3]
    per_z = X_SIZE * block
    for index in range(HEAD_SIZE):
        term = product(grads_t[index], att, NN).astype(BF16)
        for part in range(COLS // per_z):
            for x in range(X_SIZE):
                start = part * per_z + x * block
                z = index * (COLS // per_z) + part
                x_terms[z, x] = term[start : start + block, :x_cols]
                z_terms[z, x] = term[start : start + block, x_cols:]
    x_copies = []
    for step in range(1, X_SIZE):
        x_copies.append(
            send(
                x_terms.at[:, x_peer(step)],
                x_in.at[step - 1],
                x_sems.at[0, step - 1],
                x_sems.at[1, step - 1],
                device(z_at, x_peer(step), y_at),
            )
        )
    z_first_copies = []
    for step in range(1, z_size):
        z_first_copies.append(
            send(
                z_terms.at[z_peer(step)],
                z_first_in.at[step - 1],
                z_first_sems.at[0, step - 1],
                z_first_sems.at[1, step - 1],
                device(z_peer(step), x_at, y_at),
            )
        )
    for at, index in enumerate((2 * (1 - high) + 1 - core, 2 * high + 1 - core)):
        proj_send[at] = projection(index).astype(BF16)
        send(proj_send.at[at], proj_in.at[at], proj_send_sems.at[at], proj_recv_sems.at[at], sibling)
    proj_keep[0] = projection(own_across)
    proj_keep[1] = projection(own)

    for j in range(2):
        swap_wait(DO, j, do_in.at[j])
        turn(do_in, do_tr, j)
    for i in range(2):
        pl.loop(0, 3)(functools.partial(backward_unit, i))
        pack_turned(dq_tr, DQ, i)
        swap_start(DQ, i, packs.at[DQ, i], dq_in.at[y_low])
        if i == 0:
            remote(proj_send.at[0], proj_in.at[0], proj_send_sems.at[0], proj_recv_sems.at[0], sibling).wait_recv()
            hip_send[...] = (proj_keep[0] + proj_in[0].astype(F32)).astype(BF16)
            hip_copy = send(hip_send, hip_in, proj_send_sems.at[2], proj_recv_sems.at[2], across)

    accs = (dk_acc, dv_acc)

    def term_copy(at, j):
        return remote(
            near_send.at[at, j], near_in.at[at, j], term_sems.at[0, at, j], term_sems.at[1, at, j], sibling
        )

    def back_copy(at, j, target):
        return remote(
            back_send.at[at, j], back_in.at[at, j], back_sems.at[0, at, j], back_sems.at[1, at, j], target
        )

    def send_back(summed):
        for at in range(2):
            for j in range(2):
                tile = accs[at][0, j]
                third = fold(accs[at][1, j])
                if summed:
                    term_copy(at, j).wait_recv()
                    tile += near_in[at, j, :SPAN].astype(F32)
                    third += near_in[at, j, SPAN:].astype(F32)
                back_send[at, j, :SPAN] = tile.astype(BF16)
                back_send[at, j, SPAN:] = third.astype(BF16)
                pl.when(has_before)(back_copy(at, j, before).start)

    for at in range(2):
        for j in range(2):
            near_send[at, j, :SPAN] = accs[at][0, 2 + j].astype(BF16)
            near_send[at, j, SPAN:] = fold(accs[at][1, 2 + j]).astype(BF16)
            copy = term_copy(at, j)
            copy.start()
            started.append(copy)
            waits.append((has_before, back_copy(at, j, before).wait_send))
    pl.when(core == 0)(functools.partial(send_back, False))
    pl.when(core == 1)(functools.partial(send_back, True))

    for copy in x_copies:
        copy.wait_recv()
    for z in range(z_size):
        total = x_terms[z, x_at].astype(F32)
        for step in range(1, X_SIZE):
            total += x_in[step - 1, z].astype(F32)
        z_send[z] = total.astype(BF16)
    z_copies = []
    for step in range(1, z_size):
        z_copies.append(
            send(
                z_send.at[z_peer(step)],
                z_in.at[step - 1],
                z_sems.at[0, step - 1],
                z_sems.at[1, step - 1],
                device(z_peer(step), x_at, y_at),
            )
        )
    for copy in z_first_copies:
        copy.wait_recv()
    for x in range(X_SIZE):
        total = z_terms[z_at, x].astype(F32)
        for step in range(1, z_size):
            total += z_first_in[step - 1, x].astype(F32)
        x_send[x] = total.astype(BF16)
    x_last_copies = []
    for step in range(1, X_SIZE):
        x_last_copies.append(
            send(
                x_send.at[x_peer(step)],
                x_last_in.at[step - 1],
                x_last_sems.at[0, step - 1],
                x_last_sems.at[1, step - 1],
                device(z_at, x_peer(step), y_at),
            )
        )

    def finish(near):
        for at in range(2):
            for j in range(2):
                tile = accs[at][0, 4 + j]
                third = fold(accs[at][1, 4 + j])
                if near:
                    term_copy(at, j).wait_recv()
                    tile += near_in[at, j, :SPAN].astype(F32)
                    third += near_in[at, j, SPAN:].astype(F32)
                pl.when(has_after)(back_copy(at, j, after).wait_recv)
                tile += back_in[at, j, :SPAN].astype(F32)
                third += back_in[at, j, SPAN:].astype(F32)
                kind = (DK, DV)[at]
                packs[kind, j, :SPAN] = tile.astype(BF16)
                packs[kind, j, SPAN:] = third.astype(BF16)
                swap_start(kind, j, packs.at[kind, j], (dk_in, dv_in)[at].at[y_low])

    finish_waits = len(waits)
    pl.when(core == 0)(functools.partial(finish, True))
    del waits[finish_waits:]
    pl.when(core == 1)(functools.partial(finish, False))
    del waits[finish_waits:]
    for kind, buffer in ((DK, dk_in), (DV, dv_in)):
        for j in range(2):
            src = packs.at[kind, j]
            copy = remote(src, src, a2a_send_sems.at[kind, j], a2a_recv_sems.at[kind, y_low], partners[j])
            waits.append((jnp.logical_not(is_self[j]), copy.wait_send))

    for copy in z_copies:
        copy.wait_recv()
    sums[:, :x_cols] = z_send[z_at].astype(F32)
    for step in range(1, z_size):
        sums[:, :x_cols] += z_in[step - 1].astype(F32)
    for copy in x_last_copies:
        copy.wait_recv()
    sums[:, x_cols:] = x_send[x_at].astype(F32)
    for step in range(1, X_SIZE):
        sums[:, x_cols:] += x_last_in[step - 1].astype(F32)
    out_rows = dw_ref.shape[0]
    for piece in range(Y_SIZE):
        y_send[piece, 0:out_rows] = sums[piece * out_rows : (piece + 1) * out_rows]
    y_copies = []
    for step in range(1, Y_SIZE):
        y_copies.append(
            send(
                y_send.at[y_peer(step)],
                y_in.at[step - 1],
                y_sems.at[0, step - 1],
                y_sems.at[1, step - 1],
                device(z_at, x_at, y_peer(step)),
            )
        )

    for j in range(2):
        swap_wait(DQ, j, dq_in.at[j])
    from_pieces(dq_in, dq_ref)
    store(dq_ref, dq_out)
    remote(proj_send.at[1], proj_in.at[1], proj_send_sems.at[1], proj_recv_sems.at[1], sibling).wait_recv()
    hip_copy.wait_recv()
    proj_ref[...] = (proj_keep[1] + proj_in[1].astype(F32) + hip_in[...].astype(F32)).astype(BF16)
    store(proj_ref, proj_out)
    for j in range(2):
        swap_wait(DK, j, dk_in.at[j])
    from_pieces(dk_in, dk_ref)
    store(dk_ref, dk_out)
    for j in range(2):
        swap_wait(DV, j, dv_in.at[j])
    from_pieces(dv_in, dv_ref)
    store(dv_ref, dv_out)
    result = y_send[y_at]
    for step in range(1, Y_SIZE):
        y_copies[step - 1].wait_recv()
        result += y_in[step - 1]
    dw_ref[...] = result[0:out_rows]
    store(dw_ref, dw_out)

    for copy in started:
        copy.wait_send()
    for sent, wait in waits:
        pl.when(sent)(wait)
    for copy in stores:
        copy.wait()


def results_kernel(*refs):
    sems = refs[-1]
    count = (len(refs) - 1) // 2
    copies = [pltpu.make_async_copy(refs[at], refs[count + at], sems.at[at]) for at in range(count)]
    for copy in copies:
        copy.start()
    for copy in copies:
        copy.wait()


def shards(query_rows, key_rows, value_rows, out_weight, out_grad):
    seq_size = lax.axis_size("seq")
    z_size = seq_size // (X_SIZE * Y_SIZE)
    out_rows = out_weight.shape[0] // seq_size
    block = out_rows * Y_SIZE
    padded = (out_rows + 7) // 8 * 8
    x_cols = 2 * LANES
    rows_out = jax.ShapeDtypeStruct((SPAN, COLS), BF16)
    vmem = pltpu.VMEM
    dma = pltpu.SemaphoreType.DMA
    piece = (PIECE, LANES)
    scratch = [
        vmem((SPAN, COLS), BF16),
        vmem((SPAN, COLS), BF16),
        vmem((SPAN, COLS), BF16),
        vmem((SPAN, COLS), BF16),
        vmem((out_rows, COLS), F32),
        vmem((SPAN, COLS), BF16),
        vmem((SPAN, COLS), BF16),
        vmem((SPAN, COLS), BF16),
        vmem(out_weight.shape, BF16),
        vmem((8, 2) + piece, BF16),
        vmem((2,) + piece, BF16),
        vmem((2,) + piece, BF16),
        vmem((SLOTS,) + piece, BF16),
        vmem((SLOTS,) + piece, BF16),
        vmem((2,) + piece, BF16),
        vmem((2,) + piece, BF16),
        vmem((2,) + piece, BF16),
        vmem((2,) + piece, BF16),
        vmem((HEAD_SIZE, SPAN, COLS), BF16),
        vmem((HEAD_SIZE, COLS, SPAN), BF16),
        vmem((2, SLOTS, SPAN, LANES), BF16),
        vmem((2, SLOTS, SPAN, LANES), BF16),
        vmem((2, SLOTS, LANES, SPAN), BF16),
        vmem((2, SLOTS, LANES, SPAN), BF16),
        vmem((6, LANES, SPAN), BF16),
        vmem((6, LANES, SPAN), BF16),
        vmem((WINDOW, SPAN, SPAN), F32),
        vmem((6, WINDOW, SPAN, SPAN), BF16),
        vmem((6, 1, SPAN), F32),
        vmem((2, 2, LANES, SPAN), F32),
        vmem((2, 2, LANES, SPAN), F32),
        vmem((2, SLOTS, SPAN, LANES), F32),
        vmem((2, SLOTS, SPAN, LANES), F32),
        vmem((2, 2) + piece, BF16),
        vmem((2, 2) + piece, BF16),
        vmem((2, 2) + piece, BF16),
        vmem((2, 2) + piece, BF16),
        vmem((SPAN, COLS), BF16),
        vmem((2, SPAN, COLS), BF16),
        vmem((2, SPAN, COLS), BF16),
        vmem((2, SPAN, COLS), F32),
        vmem((SPAN, COLS), BF16),
        vmem((SPAN, COLS), BF16),
        vmem((z_size, X_SIZE, block, x_cols), BF16),
        vmem((X_SIZE - 1, z_size, block, x_cols), BF16),
        vmem((z_size, block, x_cols), BF16),
        vmem((z_size - 1, block, x_cols), BF16),
        vmem((z_size, X_SIZE, block, COLS - x_cols), BF16),
        vmem((z_size - 1, X_SIZE, block, COLS - x_cols), BF16),
        vmem((X_SIZE, block, COLS - x_cols), BF16),
        vmem((X_SIZE - 1, block, COLS - x_cols), BF16),
        vmem((Y_SIZE, padded, COLS), F32),
        vmem((Y_SIZE - 1, padded, COLS), F32),
        vmem((block, COLS), F32),
        dma((5,)),
        dma((5,)),
        dma((8, 2)),
        dma((8, 2)),
        dma((2, 2, 2)),
        dma((2, 2, 2)),
        dma((2, 2, 2)),
        dma((2, 2, 2)),
        dma((3,)),
        dma((3,)),
        dma((3,)),
        dma((3,)),
        dma((2, X_SIZE - 1)),
        dma((2, z_size - 1)),
        dma((2, z_size - 1)),
        dma((2, X_SIZE - 1)),
        dma((2, Y_SIZE - 1)),
    ]
    outputs = (rows_out,) * 4 + (jax.ShapeDtypeStruct((out_rows, COLS), F32),)
    anywhere = pl.BlockSpec(memory_space=pl.ANY)
    results = pl.pallas_call(
        functools.partial(layer_kernel, z_size),
        out_shape=outputs,
        in_specs=[anywhere] * 5,
        out_specs=(anywhere,) * 5,
        scratch_shapes=scratch,
        compiler_params=pltpu.CompilerParams(
            collective_id=0, has_side_effects=True, vmem_limit_bytes=53 * 1024 * 1024
        ),
    )(query_rows, key_rows, value_rows, out_weight, out_grad)
    return pl.pallas_call(
        results_kernel,
        out_shape=outputs,
        in_specs=[pl.BlockSpec(memory_space=pltpu.VMEM)] * 5,
        out_specs=(anywhere,) * 5,
        scratch_shapes=[dma((5,))],
        compiler_params=pltpu.CompilerParams(vmem_limit_bytes=4 * 1024 * 1024),
    )(*results)


def solution(mesh):
    in_specs = (
        P("seq", "head"),
        P("seq", "head"),
        P("seq", "head"),
        P(None, "head"),
        P("seq", "head"),
    )
    out_specs = (
        P("seq", "head"),
        P("seq", "head"),
        P("seq", "head"),
        P("seq", "head"),
        P("seq", "head"),
    )
    return jax.shard_map(shards, mesh=mesh, in_specs=in_specs, out_specs=out_specs, check_vma=False)
```

```python
import functools

import jax
import jax.numpy as jnp
from jax import lax
from jax.experimental import pallas as pl
from jax.experimental.pallas import tpu as pltpu
from jax.sharding import PartitionSpec as P

MESH = pl.DeviceIdType.MESH
BF16 = jnp.bfloat16
F32 = jnp.float32
SPAN = 256
COLS = 384
HEAD_DIM = 64
LANES = 128
HALF = 128
PIECE = SPAN + HALF
SLOTS = 6
WINDOW = 5
X_SIZE = 4
Y_SIZE = 4
HEAD_SIZE = 4
NN = (((1,), (0,)), ((), ()))
NT = (((1,), (1,)), ((), ()))
K, Q, V, DO, ATT, DQ, DK, DV = range(8)


def product(left, right, dims):
    return lax.dot_general(left, right, dims, preferred_element_type=F32)


def low_lanes(rows):
    return lax.broadcasted_iota(jnp.int32, (rows, LANES), 1) < HEAD_DIM


def swap(block):
    return pltpu.roll(block, HEAD_DIM, 1)


def fold(block):
    return jnp.where(low_lanes(HALF), block[:HALF], swap(block[HALF:]))


def to_pieces(tiles, piece_ref, scale=None):
    first, middle, last = [tile.astype(F32) for tile in tiles]
    if scale is not None:
        first, middle, last = first * scale, middle * scale, last * scale
    swapped = swap(middle)
    piece_ref[0, :SPAN] = first.astype(BF16)
    piece_ref[0, SPAN:] = jnp.where(low_lanes(HALF), middle[:HALF], swapped[HALF:]).astype(BF16)
    piece_ref[1, :SPAN] = last.astype(BF16)
    piece_ref[1, SPAN:] = jnp.where(low_lanes(HALF), swapped[:HALF], middle[HALF:]).astype(BF16)


def from_pieces(piece_ref, out_ref):
    out_ref[:, 0:LANES] = piece_ref[0, :SPAN]
    out_ref[:, 2 * LANES : 3 * LANES] = piece_ref[1, :SPAN]
    low = piece_ref[0, SPAN:].astype(F32)
    high = piece_ref[1, SPAN:].astype(F32)
    top = jnp.where(low_lanes(HALF), low, swap(high))
    bottom = jnp.where(low_lanes(HALF), swap(low), high)
    out_ref[:HALF, LANES : 2 * LANES] = top.astype(BF16)
    out_ref[HALF:, LANES : 2 * LANES] = bottom.astype(BF16)


def unfold(third):
    wide = third.astype(F32)
    return jnp.concatenate([wide, swap(wide)], axis=0)


def layer_kernel(
    z_size,
    q_hbm, k_hbm, v_hbm, w_hbm, g_hbm,
    proj_ref, dq_ref, dk_ref, dv_ref, dw_ref,
    q_ref, k_ref, v_ref, w_ref, packs, q_in, do_in, k_in, v_in, att_in, dq_in, dk_in, dv_in,
    grads, grads_t, k_nat, v_nat, k_tr, v_tr, q_tr, do_tr,
    scores, weights, inverse, att_tr, dq_tr, dk_acc, dv_acc,
    near_send, near_in, back_send, back_in, attended,
    proj_send, proj_in, proj_keep, hip_send, hip_in,
    x_terms, x_in, z_send, z_in, z_terms, z_first_in, x_send, x_last_in, y_send, y_in, sums,
    load_sems, a2a_send_sems, a2a_recv_sems, flow_sems, near_sems, back_sems, term_sems,
    grad_send_sems, grad_recv_sems, proj_send_sems, proj_recv_sems, x_sems, z_sems, z_first_sems, x_last_sems, y_sems,
):
    seq = lax.axis_index("seq")
    head = lax.axis_index("head")
    rows = z_size * X_SIZE
    y_at = seq % Y_SIZE
    row_at = seq // Y_SIZE
    x_at = row_at % X_SIZE
    z_at = row_at // X_SIZE
    core = head % 2
    high = head // 2
    y_half = y_at // 2
    y_low = y_at % 2

    def at_row(row):
        return (row % rows) * Y_SIZE + y_at

    partners = [(row_at * Y_SIZE + 2 * core + j, 2 * high + y_half) for j in range(2)]
    is_self = [(y_half == core) & (y_low == j) for j in range(2)]
    other = 2 * high + 1 - core
    after = (at_row(row_at + 1), head)
    before = (at_row(row_at + rows - 1), head)
    sibling = (seq, other)
    across = (seq, 2 * (1 - high) + core)

    has_after = row_at < rows - 1
    has_before = row_at > 0

    def x_peer(step):
        return (x_at + step) % X_SIZE

    def z_peer(step):
        return (z_at + step) % z_size

    def y_peer(step):
        return (y_at + step) % Y_SIZE

    def device(z, x, y):
        return ((z * X_SIZE + x) * Y_SIZE + y, head)

    barrier = pltpu.get_barrier_semaphore()

    def greet(target):
        pl.semaphore_signal(barrier, inc=1, device_id=target, device_id_type=MESH)

    for j in range(2):
        pl.when(jnp.logical_not(is_self[j]))(functools.partial(greet, partners[j]))
    pl.when(has_after)(functools.partial(greet, after))
    pl.when(has_before)(functools.partial(greet, before))
    greet(sibling)
    greet(across)
    for step in range(1, X_SIZE):
        greet(device(z_at, x_peer(step), y_at))
    for step in range(1, z_size):
        greet(device(z_peer(step), x_at, y_at))
    for step in range(1, Y_SIZE):
        greet(device(z_at, x_at, y_peer(step)))

    def tiles_of(ref):
        return [ref[:, t * LANES : (t + 1) * LANES] for t in range(3)]

    loads = {}
    for at, (name, src, dst) in enumerate(
        (("k", k_hbm, k_ref), ("v", v_hbm, v_ref), ("q", q_hbm, q_ref), ("g", g_hbm, grads.at[head]), ("w", w_hbm, w_ref))
    ):
        loads[name] = pltpu.make_async_copy(src, dst, load_sems.at[at])
        loads[name].start()
    loads["k"].wait()
    to_pieces(tiles_of(k_ref), packs.at[K])
    loads["v"].wait()
    to_pieces(tiles_of(v_ref), packs.at[V])
    loads["q"].wait()
    to_pieces(tiles_of(q_ref), packs.at[Q], HEAD_DIM**-0.5)
    loads["g"].wait()

    @pl.when(jnp.logical_not(has_before))
    def _():
        k_in[0:2] = jnp.zeros((2, PIECE, LANES), BF16)
        v_in[0:2] = jnp.zeros((2, PIECE, LANES), BF16)

    @pl.when(jnp.logical_not(has_before) & (core == 0))
    def _():
        k_in[2:4] = jnp.zeros((2, PIECE, LANES), BF16)
        v_in[2:4] = jnp.zeros((2, PIECE, LANES), BF16)

    @pl.when(jnp.logical_not(has_after))
    def _():
        back_in[...] = jnp.zeros(back_in.shape, BF16)

    greeted = X_SIZE + Y_SIZE + z_size - 3 + 6 - jnp.where(y_half == core, 1, 0)
    greeted -= jnp.where(has_after, 0, 1) + jnp.where(has_before, 0, 1)
    pl.semaphore_wait(barrier, greeted)

    started = []

    def remote(src, dst, send_sem, recv_sem, target):
        return pltpu.make_async_remote_copy(
            src_ref=src, dst_ref=dst, send_sem=send_sem, recv_sem=recv_sem, device_id=target, device_id_type=MESH
        )

    def send(*args):
        copy = remote(*args)
        copy.start()
        started.append(copy)
        return copy

    waits = []

    def swap_start(kind, j, src, dst):
        copy = remote(src, dst, a2a_send_sems.at[kind, j], a2a_recv_sems.at[kind, y_low], partners[j])
        pl.when(jnp.logical_not(is_self[j]))(copy.start)
        pl.when(is_self[j])(pltpu.make_async_copy(src, dst, a2a_recv_sems.at[kind, y_low]).start)
        waits.append((jnp.logical_not(is_self[j]), copy.wait_send))

    def swap_wait(kind, j, dst):
        remote(dst, dst, a2a_send_sems.at[kind, j], a2a_recv_sems.at[kind, j], partners[j]).wait_recv()

    def grad_send(index, step, target):
        return send(grads.at[index], grads.at[index], grad_send_sems.at[step - 1], grad_recv_sems.at[step - 1], target)

    own = head
    own_across = 2 * (1 - high) + core
    from_step = {1: other, 2: own_across, 3: 2 * (1 - high) + 1 - core}

    def grad_wait(step):
        slot = grads.at[from_step[step]]
        remote(slot, slot, grad_send_sems.at[step - 1], grad_recv_sems.at[step - 1], across).wait_recv()

    for kind, buffer in ((K, k_in), (V, v_in)):
        for j in range(2):
            swap_start(kind, j, packs.at[kind, j], buffer.at[4 + y_low])
    for j in range(2):
        swap_start(Q, j, packs.at[Q, j], q_in.at[y_low])

    def near_copy(at, buffer, slot, j):
        return remote(
            buffer.at[slot + j], buffer.at[2 + j], near_sems.at[0, at, j], near_sems.at[1, at, j], sibling
        )

    def far_copy(at, buffer, j):
        return remote(buffer.at[4 + j], buffer.at[j], flow_sems.at[0, at, j], flow_sems.at[1, at, j], after)

    def flow(at, kind, buffer):
        for j in range(2):
            swap_wait(kind, j, buffer.at[4 + j])
            far = far_copy(at, buffer, j)
            pl.when(has_after)(far.start)
            waits.append((has_after, far.wait_send))
            near = near_copy(at, buffer, 4, j)
            pl.when(core == 0)(near.start)
            waits.append(((core == 0) | has_before, near.wait_send))

    def flow_on(at, buffer):
        for j in range(2):
            pl.when(has_before)(
                remote(buffer.at[j], buffer.at[j], flow_sems.at[0, at, j], flow_sems.at[1, at, j], before).wait_recv
            )
            pl.when((core == 1) & has_before)(near_copy(at, buffer, 0, j).start)

    def near_wait(at, buffer):
        for j in range(2):
            pl.when((core == 1) | has_before)(near_copy(at, buffer, 2, j).wait_recv)

    def spread(buffer, natural, turned, slot):
        first = buffer[slot, :SPAN]
        third = unfold(buffer[slot, SPAN:])
        natural[0, slot] = first
        natural[1, slot] = third.astype(BF16)
        turned[0, slot] = first.astype(F32).T.astype(BF16)
        turned[1, slot] = third.T.astype(BF16)

    def turn(buffer, turned, j):
        first = buffer[j, :SPAN].astype(F32).T
        third = unfold(buffer[j, SPAN:]).T
        upper = lax.broadcasted_iota(jnp.int32, (LANES, SPAN), 0) < HEAD_DIM
        turned[3 * j] = jnp.where(upper, first, 0.0).astype(BF16)
        turned[3 * j + 1] = jnp.where(upper, 0.0, first).astype(BF16)
        turned[3 * j + 2] = jnp.where(upper, third, 0.0).astype(BF16)

    flow(0, K, k_in)
    flow(1, V, v_in)
    grad_send(own, 2, across)
    grad_send(own, 1, sibling)
    for slot in (4, 5):
        spread(k_in, k_nat, k_tr, slot)
        spread(v_in, v_nat, v_tr, slot)
    for j in range(2):
        swap_wait(Q, j, q_in.at[j])
        turn(q_in, q_tr, j)
    flow_on(0, k_in)
    for slot in (0, 1):
        spread(k_in, k_nat, k_tr, slot)
    flow_on(1, v_in)
    near_wait(0, k_in)
    for slot in (2, 3):
        spread(k_in, k_nat, k_tr, slot)
    for slot in (0, 1):
        spread(v_in, v_nat, v_tr, slot)
    near_wait(1, v_in)
    for slot in (2, 3):
        spread(v_in, v_nat, v_tr, slot)

    def seen(slot):
        return (row_at > 0) | (slot >= 4 - 2 * core)

    def place(i, h):
        return h // 2, pl.multiple_of((h % 2) * HEAD_DIM, HEAD_DIM), 3 * i + h

    def forward_unit(i, h):
        tile, first, unit = place(i, h)
        query = q_tr[unit]
        top = None
        for j in range(WINDOW):
            block = product(k_nat[tile, i + j], query, NN)
            block = jnp.where(seen(i + j), block, -1e30)
            scores[j] = block
            peak = jnp.max(block, axis=0, keepdims=True)
            top = peak if top is None else jnp.maximum(top, peak)
        total = jnp.zeros((1, SPAN), F32)
        acc = jnp.zeros((HEAD_DIM, SPAN), F32)
        for j in range(WINDOW):
            part = jnp.exp(scores[j] - top)
            total += jnp.sum(part, axis=0, keepdims=True)
            part = part.astype(BF16)
            weights[unit, j] = part
            acc += product(v_tr[tile, i + j, pl.ds(first, HEAD_DIM), :], part, NN)
        share = 1.0 / total
        inverse[unit] = share
        att_tr[i, tile, pl.ds(first, HEAD_DIM), :] = acc * share

    def pack_turned(turned, kind, i):
        packs[kind, i, :SPAN] = turned[i, 0].T.astype(BF16)
        packs[kind, i, SPAN:] = fold(turned[i, 1].T).astype(BF16)

    for i in range(2):
        att_tr[i, 1] = jnp.zeros((LANES, SPAN), F32)
        dq_tr[i, 1] = jnp.zeros((LANES, SPAN), F32)
    dk_acc[...] = jnp.zeros(dk_acc.shape, F32)
    dv_acc[...] = jnp.zeros(dv_acc.shape, F32)

    def forward(i):
        pl.loop(0, 3)(functools.partial(forward_unit, i))
        pack_turned(att_tr, ATT, i)
        swap_start(ATT, i, packs.at[ATT, i], att_in.at[y_low])

    forward(0)
    grad_wait(2)
    grad_send(own_across, 3, sibling)
    forward(1)
    loads["w"].wait()
    grad_wait(1)
    grad_wait(3)
    acc = product(grads[0], w_ref[0:COLS], NN)
    for index in range(1, HEAD_SIZE):
        acc += product(grads[index], w_ref[index * COLS : (index + 1) * COLS], NN)
    to_pieces([acc[:, t * LANES : (t + 1) * LANES] for t in range(3)], packs.at[DO])
    for j in range(2):
        swap_start(DO, j, packs.at[DO, j], do_in.at[y_low])
    for index in range(HEAD_SIZE):
        grads_t[index] = grads[index].astype(F32).T.astype(BF16)

    def backward_unit(i, h):
        tile, first, unit = place(i, h)
        query = q_tr[unit]
        d_out = (do_tr[unit].astype(F32) * inverse[unit]).astype(BF16)
        do_tr[unit] = d_out
        d_half = do_tr[unit, pl.ds(first, HEAD_DIM), :].astype(F32)
        att_half = att_tr[i, tile, pl.ds(first, HEAD_DIM), :].astype(BF16).astype(F32)
        delta = jnp.sum(d_half * att_half, axis=0, keepdims=True)
        acc = jnp.zeros((HEAD_DIM, SPAN), F32)
        for j in range(WINDOW):
            part = weights[unit, j]
            d_part = product(v_nat[tile, i + j], d_out, NN)
            d_score = (part.astype(F32) * (d_part - delta)).astype(BF16)
            dk_acc[tile, i + j] += product(d_score, query, NT)
            dv_acc[tile, i + j] += product(part, d_out, NT)
            acc += product(k_tr[tile, i + j, pl.ds(first, HEAD_DIM), :], d_score, NN)
        dq_tr[i, tile, pl.ds(first, HEAD_DIM), :] = acc * (HEAD_DIM**-0.5)

    for j in range(2):
        swap_wait(ATT, j, att_in.at[j])
    from_pieces(att_in, attended)
    att = attended[...]

    def projection(index):
        weight = w_ref[pl.ds(pl.multiple_of(index * COLS, COLS), COLS), :]
        return product(att, weight, NT)

    block = x_terms.shape[2]
    x_cols = x_terms.shape[3]
    per_z = X_SIZE * block
    for index in range(HEAD_SIZE):
        term = product(grads_t[index], att, NN).astype(BF16)
        for part in range(COLS // per_z):
            for x in range(X_SIZE):
                start = part * per_z + x * block
                z = index * (COLS // per_z) + part
                x_terms[z, x] = term[start : start + block, :x_cols]
                z_terms[z, x] = term[start : start + block, x_cols:]
    x_copies = []
    for step in range(1, X_SIZE):
        x_copies.append(
            send(
                x_terms.at[:, x_peer(step)],
                x_in.at[step - 1],
                x_sems.at[0, step - 1],
                x_sems.at[1, step - 1],
                device(z_at, x_peer(step), y_at),
            )
        )
    z_first_copies = []
    for step in range(1, z_size):
        z_first_copies.append(
            send(
                z_terms.at[z_peer(step)],
                z_first_in.at[step - 1],
                z_first_sems.at[0, step - 1],
                z_first_sems.at[1, step - 1],
                device(z_peer(step), x_at, y_at),
            )
        )
    for at, index in enumerate((2 * (1 - high) + 1 - core, 2 * high + 1 - core)):
        proj_send[at] = projection(index).astype(BF16)
        send(proj_send.at[at], proj_in.at[at], proj_send_sems.at[at], proj_recv_sems.at[at], sibling)
    proj_keep[0] = projection(own_across)
    proj_keep[1] = projection(own)

    for j in range(2):
        swap_wait(DO, j, do_in.at[j])
        turn(do_in, do_tr, j)
    for i in range(2):
        pl.loop(0, 3)(functools.partial(backward_unit, i))
        pack_turned(dq_tr, DQ, i)
        swap_start(DQ, i, packs.at[DQ, i], dq_in.at[y_low])
        if i == 0:
            remote(proj_send.at[0], proj_in.at[0], proj_send_sems.at[0], proj_recv_sems.at[0], sibling).wait_recv()
            hip_send[...] = (proj_keep[0] + proj_in[0].astype(F32)).astype(BF16)
            hip_copy = send(hip_send, hip_in, proj_send_sems.at[2], proj_recv_sems.at[2], across)

    accs = (dk_acc, dv_acc)

    def term_copy(at, j):
        return remote(
            near_send.at[at, j], near_in.at[at, j], term_sems.at[0, at, j], term_sems.at[1, at, j], sibling
        )

    def back_copy(at, j, target):
        return remote(
            back_send.at[at, j], back_in.at[at, j], back_sems.at[0, at, j], back_sems.at[1, at, j], target
        )

    def send_back(summed):
        for at in range(2):
            for j in range(2):
                tile = accs[at][0, j]
                third = fold(accs[at][1, j])
                if summed:
                    term_copy(at, j).wait_recv()
                    tile += near_in[at, j, :SPAN].astype(F32)
                    third += near_in[at, j, SPAN:].astype(F32)
                back_send[at, j, :SPAN] = tile.astype(BF16)
                back_send[at, j, SPAN:] = third.astype(BF16)
                pl.when(has_before)(back_copy(at, j, before).start)

    for at in range(2):
        for j in range(2):
            near_send[at, j, :SPAN] = accs[at][0, 2 + j].astype(BF16)
            near_send[at, j, SPAN:] = fold(accs[at][1, 2 + j]).astype(BF16)
            copy = term_copy(at, j)
            copy.start()
            started.append(copy)
            waits.append((has_before, back_copy(at, j, before).wait_send))
    pl.when(core == 0)(functools.partial(send_back, False))
    pl.when(core == 1)(functools.partial(send_back, True))

    for copy in x_copies:
        copy.wait_recv()
    for z in range(z_size):
        total = x_terms[z, x_at].astype(F32)
        for step in range(1, X_SIZE):
            total += x_in[step - 1, z].astype(F32)
        z_send[z] = total.astype(BF16)
    z_copies = []
    for step in range(1, z_size):
        z_copies.append(
            send(
                z_send.at[z_peer(step)],
                z_in.at[step - 1],
                z_sems.at[0, step - 1],
                z_sems.at[1, step - 1],
                device(z_peer(step), x_at, y_at),
            )
        )
    for copy in z_first_copies:
        copy.wait_recv()
    for x in range(X_SIZE):
        total = z_terms[z_at, x].astype(F32)
        for step in range(1, z_size):
            total += z_first_in[step - 1, x].astype(F32)
        x_send[x] = total.astype(BF16)
    x_last_copies = []
    for step in range(1, X_SIZE):
        x_last_copies.append(
            send(
                x_send.at[x_peer(step)],
                x_last_in.at[step - 1],
                x_last_sems.at[0, step - 1],
                x_last_sems.at[1, step - 1],
                device(z_at, x_peer(step), y_at),
            )
        )

    def finish(near):
        for at in range(2):
            for j in range(2):
                tile = accs[at][0, 4 + j]
                third = fold(accs[at][1, 4 + j])
                if near:
                    term_copy(at, j).wait_recv()
                    tile += near_in[at, j, :SPAN].astype(F32)
                    third += near_in[at, j, SPAN:].astype(F32)
                pl.when(has_after)(back_copy(at, j, after).wait_recv)
                tile += back_in[at, j, :SPAN].astype(F32)
                third += back_in[at, j, SPAN:].astype(F32)
                kind = (DK, DV)[at]
                packs[kind, j, :SPAN] = tile.astype(BF16)
                packs[kind, j, SPAN:] = third.astype(BF16)
                swap_start(kind, j, packs.at[kind, j], (dk_in, dv_in)[at].at[y_low])

    finish_waits = len(waits)
    pl.when(core == 0)(functools.partial(finish, True))
    del waits[finish_waits:]
    pl.when(core == 1)(functools.partial(finish, False))
    del waits[finish_waits:]
    for kind, buffer in ((DK, dk_in), (DV, dv_in)):
        for j in range(2):
            src = packs.at[kind, j]
            copy = remote(src, src, a2a_send_sems.at[kind, j], a2a_recv_sems.at[kind, y_low], partners[j])
            waits.append((jnp.logical_not(is_self[j]), copy.wait_send))

    for copy in z_copies:
        copy.wait_recv()
    sums[:, :x_cols] = z_send[z_at].astype(F32)
    for step in range(1, z_size):
        sums[:, :x_cols] += z_in[step - 1].astype(F32)
    for copy in x_last_copies:
        copy.wait_recv()
    sums[:, x_cols:] = x_send[x_at].astype(F32)
    for step in range(1, X_SIZE):
        sums[:, x_cols:] += x_last_in[step - 1].astype(F32)
    out_rows = dw_ref.shape[0]
    for piece in range(Y_SIZE):
        y_send[piece, 0:out_rows] = sums[piece * out_rows : (piece + 1) * out_rows]
    y_copies = []
    for step in range(1, Y_SIZE):
        y_copies.append(
            send(
                y_send.at[y_peer(step)],
                y_in.at[step - 1],
                y_sems.at[0, step - 1],
                y_sems.at[1, step - 1],
                device(z_at, x_at, y_peer(step)),
            )
        )

    for j in range(2):
        swap_wait(DQ, j, dq_in.at[j])
    from_pieces(dq_in, dq_ref)
    remote(proj_send.at[1], proj_in.at[1], proj_send_sems.at[1], proj_recv_sems.at[1], sibling).wait_recv()
    hip_copy.wait_recv()
    proj_ref[...] = (proj_keep[1] + proj_in[1].astype(F32) + hip_in[...].astype(F32)).astype(BF16)
    for j in range(2):
        swap_wait(DK, j, dk_in.at[j])
    from_pieces(dk_in, dk_ref)
    for j in range(2):
        swap_wait(DV, j, dv_in.at[j])
    from_pieces(dv_in, dv_ref)
    result = y_send[y_at]
    for step in range(1, Y_SIZE):
        y_copies[step - 1].wait_recv()
        result += y_in[step - 1]
    dw_ref[...] = result[0:out_rows]

    for copy in started:
        copy.wait_send()
    for sent, wait in waits:
        pl.when(sent)(wait)


def results_kernel(*refs):
    sems = refs[-1]
    count = (len(refs) - 1) // 2
    copies = [pltpu.make_async_copy(refs[at], refs[count + at], sems.at[at]) for at in range(count)]
    for copy in copies:
        copy.start()
    for copy in copies:
        copy.wait()


def shards(query_rows, key_rows, value_rows, out_weight, out_grad):
    seq_size = lax.axis_size("seq")
    z_size = seq_size // (X_SIZE * Y_SIZE)
    out_rows = out_weight.shape[0] // seq_size
    block = out_rows * Y_SIZE
    padded = (out_rows + 7) // 8 * 8
    x_cols = 2 * LANES
    rows_out = jax.ShapeDtypeStruct((SPAN, COLS), BF16)
    vmem = pltpu.VMEM
    dma = pltpu.SemaphoreType.DMA
    piece = (PIECE, LANES)
    scratch = [
        vmem((SPAN, COLS), BF16),
        vmem((SPAN, COLS), BF16),
        vmem((SPAN, COLS), BF16),
        vmem(out_weight.shape, BF16),
        vmem((8, 2) + piece, BF16),
        vmem((2,) + piece, BF16),
        vmem((2,) + piece, BF16),
        vmem((SLOTS,) + piece, BF16),
        vmem((SLOTS,) + piece, BF16),
        vmem((2,) + piece, BF16),
        vmem((2,) + piece, BF16),
        vmem((2,) + piece, BF16),
        vmem((2,) + piece, BF16),
        vmem((HEAD_SIZE, SPAN, COLS), BF16),
        vmem((HEAD_SIZE, COLS, SPAN), BF16),
        vmem((2, SLOTS, SPAN, LANES), BF16),
        vmem((2, SLOTS, SPAN, LANES), BF16),
        vmem((2, SLOTS, LANES, SPAN), BF16),
        vmem((2, SLOTS, LANES, SPAN), BF16),
        vmem((6, LANES, SPAN), BF16),
        vmem((6, LANES, SPAN), BF16),
        vmem((WINDOW, SPAN, SPAN), F32),
        vmem((6, WINDOW, SPAN, SPAN), BF16),
        vmem((6, 1, SPAN), F32),
        vmem((2, 2, LANES, SPAN), F32),
        vmem((2, 2, LANES, SPAN), F32),
        vmem((2, SLOTS, SPAN, LANES), F32),
        vmem((2, SLOTS, SPAN, LANES), F32),
        vmem((2, 2) + piece, BF16),
        vmem((2, 2) + piece, BF16),
        vmem((2, 2) + piece, BF16),
        vmem((2, 2) + piece, BF16),
        vmem((SPAN, COLS), BF16),
        vmem((2, SPAN, COLS), BF16),
        vmem((2, SPAN, COLS), BF16),
        vmem((2, SPAN, COLS), F32),
        vmem((SPAN, COLS), BF16),
        vmem((SPAN, COLS), BF16),
        vmem((z_size, X_SIZE, block, x_cols), BF16),
        vmem((X_SIZE - 1, z_size, block, x_cols), BF16),
        vmem((z_size, block, x_cols), BF16),
        vmem((z_size - 1, block, x_cols), BF16),
        vmem((z_size, X_SIZE, block, COLS - x_cols), BF16),
        vmem((z_size - 1, X_SIZE, block, COLS - x_cols), BF16),
        vmem((X_SIZE, block, COLS - x_cols), BF16),
        vmem((X_SIZE - 1, block, COLS - x_cols), BF16),
        vmem((Y_SIZE, padded, COLS), F32),
        vmem((Y_SIZE - 1, padded, COLS), F32),
        vmem((block, COLS), F32),
        dma((5,)),
        dma((8, 2)),
        dma((8, 2)),
        dma((2, 2, 2)),
        dma((2, 2, 2)),
        dma((2, 2, 2)),
        dma((2, 2, 2)),
        dma((3,)),
        dma((3,)),
        dma((3,)),
        dma((3,)),
        dma((2, X_SIZE - 1)),
        dma((2, z_size - 1)),
        dma((2, z_size - 1)),
        dma((2, X_SIZE - 1)),
        dma((2, Y_SIZE - 1)),
    ]
    outputs = (rows_out,) * 4 + (jax.ShapeDtypeStruct((out_rows, COLS), F32),)
    anywhere = pl.BlockSpec(memory_space=pl.ANY)
    results = pl.pallas_call(
        functools.partial(layer_kernel, z_size),
        out_shape=outputs,
        in_specs=[anywhere] * 5,
        out_specs=(pl.BlockSpec(memory_space=pltpu.VMEM),) * 5,
        scratch_shapes=scratch,
        compiler_params=pltpu.CompilerParams(
            collective_id=0, has_side_effects=True, vmem_limit_bytes=53 * 1024 * 1024
        ),
    )(query_rows, key_rows, value_rows, out_weight, out_grad)
    return pl.pallas_call(
        results_kernel,
        out_shape=outputs,
        in_specs=[pl.BlockSpec(memory_space=pltpu.VMEM)] * 5,
        out_specs=(anywhere,) * 5,
        scratch_shapes=[dma((5,))],
        compiler_params=pltpu.CompilerParams(vmem_limit_bytes=4 * 1024 * 1024),
    )(*results)


def solution(mesh):
    in_specs = (
        P("seq", "head"),
        P("seq", "head"),
        P("seq", "head"),
        P(None, "head"),
        P("seq", "head"),
    )
    out_specs = (
        P("seq", "head"),
        P("seq", "head"),
        P("seq", "head"),
        P("seq", "head"),
        P("seq", "head"),
    )
    return jax.shard_map(shards, mesh=mesh, in_specs=in_specs, out_specs=out_specs, check_vma=False)
```

```python
import functools

import jax
import jax.numpy as jnp
from jax import lax
from jax.experimental import pallas as pl
from jax.experimental.pallas import tpu as pltpu
from jax.sharding import PartitionSpec as P

MESH = pl.DeviceIdType.MESH
BF16 = jnp.bfloat16
F32 = jnp.float32
SPAN = 256
COLS = 384
HEAD_DIM = 64
LANES = 128
HALF = 128
PIECE = SPAN + HALF
SLOTS = 6
WINDOW = 5
X_SIZE = 4
Y_SIZE = 4
HEAD_SIZE = 4
NN = (((1,), (0,)), ((), ()))
NT = (((1,), (1,)), ((), ()))
K, Q, V, DO, ATT, DQ, DK, DV = range(8)


def product(left, right, dims):
    return lax.dot_general(left, right, dims, preferred_element_type=F32)


def low_lanes(rows):
    return lax.broadcasted_iota(jnp.int32, (rows, LANES), 1) < HEAD_DIM


def swap(block):
    return pltpu.roll(block, HEAD_DIM, 1)


def fold(block):
    return jnp.where(low_lanes(HALF), block[:HALF], swap(block[HALF:]))


def to_pieces(tiles, piece_ref, scale=None):
    first, middle, last = [tile.astype(F32) for tile in tiles]
    if scale is not None:
        first, middle, last = first * scale, middle * scale, last * scale
    swapped = swap(middle)
    piece_ref[0, :SPAN] = first.astype(BF16)
    piece_ref[0, SPAN:] = jnp.where(low_lanes(HALF), middle[:HALF], swapped[HALF:]).astype(BF16)
    piece_ref[1, :SPAN] = last.astype(BF16)
    piece_ref[1, SPAN:] = jnp.where(low_lanes(HALF), swapped[:HALF], middle[HALF:]).astype(BF16)


def from_pieces(piece_ref, out_ref):
    out_ref[:, 0:LANES] = piece_ref[0, :SPAN]
    out_ref[:, 2 * LANES : 3 * LANES] = piece_ref[1, :SPAN]
    low = piece_ref[0, SPAN:].astype(F32)
    high = piece_ref[1, SPAN:].astype(F32)
    top = jnp.where(low_lanes(HALF), low, swap(high))
    bottom = jnp.where(low_lanes(HALF), swap(low), high)
    out_ref[:HALF, LANES : 2 * LANES] = top.astype(BF16)
    out_ref[HALF:, LANES : 2 * LANES] = bottom.astype(BF16)


def unfold(third):
    wide = third.astype(F32)
    return jnp.concatenate([wide, swap(wide)], axis=0)


def layer_kernel(
    z_size,
    q_hbm, k_hbm, v_hbm, w_hbm, g_hbm,
    proj_ref, dq_ref, dk_ref, dv_ref, dw_ref,
    q_ref, k_ref, v_ref, w_ref, packs, q_in, do_in, k_in, v_in, att_in, dq_in, dk_in, dv_in,
    grads, grads_t, k_nat, v_nat, k_tr, v_tr, q_tr, do_tr,
    scores, weights, inverse, att_tr, dq_tr, dk_acc, dv_acc,
    near_send, near_in, back_send, back_in, attended,
    proj_send, proj_in, proj_keep, hip_send, hip_in,
    x_terms, x_in, z_send, z_in, z_terms, z_first_in, x_send, x_last_in, y_send, y_in, sums,
    load_sems, a2a_send_sems, a2a_recv_sems, flow_sems, near_sems, back_sems, term_sems,
    grad_send_sems, grad_recv_sems, proj_send_sems, proj_recv_sems, x_sems, z_sems, z_first_sems, x_last_sems, y_sems,
):
    seq = lax.axis_index("seq")
    head = lax.axis_index("head")
    rows = z_size * X_SIZE
    y_at = seq % Y_SIZE
    row_at = seq // Y_SIZE
    x_at = row_at % X_SIZE
    z_at = row_at // X_SIZE
    core = head % 2
    high = head // 2
    y_half = y_at // 2
    y_low = y_at % 2

    def at_row(row):
        return (row % rows) * Y_SIZE + y_at

    partners = [(row_at * Y_SIZE + 2 * core + j, 2 * high + y_half) for j in range(2)]
    is_self = [(y_half == core) & (y_low == j) for j in range(2)]
    other = 2 * high + 1 - core
    after = (at_row(row_at + 1), head)
    before = (at_row(row_at + rows - 1), head)
    sibling = (seq, other)
    across = (seq, 2 * (1 - high) + core)

    has_after = row_at < rows - 1
    has_before = row_at > 0

    def x_peer(step):
        return (x_at + step) % X_SIZE

    def z_peer(step):
        return (z_at + step) % z_size

    def y_peer(step):
        return (y_at + step) % Y_SIZE

    def device(z, x, y):
        return ((z * X_SIZE + x) * Y_SIZE + y, head)

    barrier = pltpu.get_barrier_semaphore()

    def greet(target):
        pl.semaphore_signal(barrier, inc=1, device_id=target, device_id_type=MESH)

    for j in range(2):
        pl.when(jnp.logical_not(is_self[j]))(functools.partial(greet, partners[j]))
    pl.when(has_after)(functools.partial(greet, after))
    pl.when(has_before)(functools.partial(greet, before))
    greet(sibling)
    greet(across)
    for step in range(1, X_SIZE):
        greet(device(z_at, x_peer(step), y_at))
    for step in range(1, z_size):
        greet(device(z_peer(step), x_at, y_at))
    for step in range(1, Y_SIZE):
        greet(device(z_at, x_at, y_peer(step)))

    def tiles_of(ref):
        return [ref[:, t * LANES : (t + 1) * LANES] for t in range(3)]

    loads = {}
    for at, (name, src, dst) in enumerate(
        (("k", k_hbm, k_ref), ("v", v_hbm, v_ref), ("q", q_hbm, q_ref), ("g", g_hbm, grads.at[head]), ("w", w_hbm, w_ref))
    ):
        loads[name] = pltpu.make_async_copy(src, dst, load_sems.at[at])
        loads[name].start()
    loads["k"].wait()
    to_pieces(tiles_of(k_ref), packs.at[K])
    @pl.when(jnp.logical_not(has_before))
    def _():
        k_in[0:2] = jnp.zeros((2, PIECE, LANES), BF16)
        v_in[0:2] = jnp.zeros((2, PIECE, LANES), BF16)

    @pl.when(jnp.logical_not(has_before) & (core == 0))
    def _():
        k_in[2:4] = jnp.zeros((2, PIECE, LANES), BF16)
        v_in[2:4] = jnp.zeros((2, PIECE, LANES), BF16)

    @pl.when(jnp.logical_not(has_after))
    def _():
        back_in[...] = jnp.zeros(back_in.shape, BF16)

    greeted = X_SIZE + Y_SIZE + z_size - 3 + 6 - jnp.where(y_half == core, 1, 0)
    greeted -= jnp.where(has_after, 0, 1) + jnp.where(has_before, 0, 1)
    pl.semaphore_wait(barrier, greeted)

    started = []

    def remote(src, dst, send_sem, recv_sem, target):
        return pltpu.make_async_remote_copy(
            src_ref=src, dst_ref=dst, send_sem=send_sem, recv_sem=recv_sem, device_id=target, device_id_type=MESH
        )

    def send(*args):
        copy = remote(*args)
        copy.start()
        started.append(copy)
        return copy

    waits = []

    def swap_start(kind, j, src, dst):
        copy = remote(src, dst, a2a_send_sems.at[kind, j], a2a_recv_sems.at[kind, y_low], partners[j])
        pl.when(jnp.logical_not(is_self[j]))(copy.start)
        pl.when(is_self[j])(pltpu.make_async_copy(src, dst, a2a_recv_sems.at[kind, y_low]).start)
        waits.append((jnp.logical_not(is_self[j]), copy.wait_send))

    def swap_wait(kind, j, dst):
        remote(dst, dst, a2a_send_sems.at[kind, j], a2a_recv_sems.at[kind, j], partners[j]).wait_recv()

    def grad_send(index, step, target):
        return send(grads.at[index], grads.at[index], grad_send_sems.at[step - 1], grad_recv_sems.at[step - 1], target)

    own = head
    own_across = 2 * (1 - high) + core
    from_step = {1: other, 2: own_across, 3: 2 * (1 - high) + 1 - core}

    def grad_wait(step):
        slot = grads.at[from_step[step]]
        remote(slot, slot, grad_send_sems.at[step - 1], grad_recv_sems.at[step - 1], across).wait_recv()

    for j in range(2):
        swap_start(K, j, packs.at[K, j], k_in.at[4 + y_low])
    loads["v"].wait()
    to_pieces(tiles_of(v_ref), packs.at[V])
    for j in range(2):
        swap_start(V, j, packs.at[V, j], v_in.at[4 + y_low])
    loads["q"].wait()
    to_pieces(tiles_of(q_ref), packs.at[Q], HEAD_DIM**-0.5)
    loads["g"].wait()
    for j in range(2):
        swap_start(Q, j, packs.at[Q, j], q_in.at[y_low])

    def near_copy(at, buffer, slot, j):
        return remote(
            buffer.at[slot + j], buffer.at[2 + j], near_sems.at[0, at, j], near_sems.at[1, at, j], sibling
        )

    def far_copy(at, buffer, j):
        return remote(buffer.at[4 + j], buffer.at[j], flow_sems.at[0, at, j], flow_sems.at[1, at, j], after)

    def flow(at, kind, buffer):
        for j in range(2):
            swap_wait(kind, j, buffer.at[4 + j])
            far = far_copy(at, buffer, j)
            pl.when(has_after)(far.start)
            waits.append((has_after, far.wait_send))
            near = near_copy(at, buffer, 4, j)
            pl.when(core == 0)(near.start)
            waits.append(((core == 0) | has_before, near.wait_send))

    def flow_on(at, buffer):
        for j in range(2):
            pl.when(has_before)(
                remote(buffer.at[j], buffer.at[j], flow_sems.at[0, at, j], flow_sems.at[1, at, j], before).wait_recv
            )
            pl.when((core == 1) & has_before)(near_copy(at, buffer, 0, j).start)

    def near_wait(at, buffer):
        for j in range(2):
            pl.when((core == 1) | has_before)(near_copy(at, buffer, 2, j).wait_recv)

    def spread(buffer, natural, turned, slot):
        first = buffer[slot, :SPAN]
        third = unfold(buffer[slot, SPAN:])
        natural[0, slot] = first
        natural[1, slot] = third.astype(BF16)
        turned[0, slot] = first.astype(F32).T.astype(BF16)
        turned[1, slot] = third.T.astype(BF16)

    def turn(buffer, turned, j):
        first = buffer[j, :SPAN].astype(F32).T
        third = unfold(buffer[j, SPAN:]).T
        upper = lax.broadcasted_iota(jnp.int32, (LANES, SPAN), 0) < HEAD_DIM
        turned[3 * j] = jnp.where(upper, first, 0.0).astype(BF16)
        turned[3 * j + 1] = jnp.where(upper, 0.0, first).astype(BF16)
        turned[3 * j + 2] = jnp.where(upper, third, 0.0).astype(BF16)

    flow(0, K, k_in)
    flow(1, V, v_in)
    grad_send(own, 2, across)
    grad_send(own, 1, sibling)
    for slot in (4, 5):
        spread(k_in, k_nat, k_tr, slot)
        spread(v_in, v_nat, v_tr, slot)
    for j in range(2):
        swap_wait(Q, j, q_in.at[j])
        turn(q_in, q_tr, j)
    flow_on(0, k_in)
    for slot in (0, 1):
        spread(k_in, k_nat, k_tr, slot)
    flow_on(1, v_in)
    near_wait(0, k_in)
    for slot in (2, 3):
        spread(k_in, k_nat, k_tr, slot)
    for slot in (0, 1):
        spread(v_in, v_nat, v_tr, slot)
    near_wait(1, v_in)
    for slot in (2, 3):
        spread(v_in, v_nat, v_tr, slot)

    def seen(slot):
        return (row_at > 0) | (slot >= 4 - 2 * core)

    def place(i, h):
        return h // 2, pl.multiple_of((h % 2) * HEAD_DIM, HEAD_DIM), 3 * i + h

    def forward_unit(i, h):
        tile, first, unit = place(i, h)
        query = q_tr[unit]
        top = None
        for j in range(WINDOW):
            block = product(k_nat[tile, i + j], query, NN)
            block = jnp.where(seen(i + j), block, -1e30)
            scores[j] = block
            peak = jnp.max(block, axis=0, keepdims=True)
            top = peak if top is None else jnp.maximum(top, peak)
        total = jnp.zeros((1, SPAN), F32)
        acc = jnp.zeros((HEAD_DIM, SPAN), F32)
        for j in range(WINDOW):
            part = jnp.exp(scores[j] - top)
            total += jnp.sum(part, axis=0, keepdims=True)
            part = part.astype(BF16)
            weights[unit, j] = part
            acc += product(v_tr[tile, i + j, pl.ds(first, HEAD_DIM), :], part, NN)
        share = 1.0 / total
        inverse[unit] = share
        att_tr[i, tile, pl.ds(first, HEAD_DIM), :] = acc * share

    def pack_turned(turned, kind, i):
        packs[kind, i, :SPAN] = turned[i, 0].T.astype(BF16)
        packs[kind, i, SPAN:] = fold(turned[i, 1].T).astype(BF16)

    for i in range(2):
        att_tr[i, 1] = jnp.zeros((LANES, SPAN), F32)
        dq_tr[i, 1] = jnp.zeros((LANES, SPAN), F32)
    dk_acc[...] = jnp.zeros(dk_acc.shape, F32)
    dv_acc[...] = jnp.zeros(dv_acc.shape, F32)

    def forward(i):
        pl.loop(0, 3)(functools.partial(forward_unit, i))
        pack_turned(att_tr, ATT, i)
        swap_start(ATT, i, packs.at[ATT, i], att_in.at[y_low])

    forward(0)
    grad_wait(2)
    grad_send(own_across, 3, sibling)
    forward(1)
    loads["w"].wait()
    grad_wait(1)
    grad_wait(3)
    acc = product(grads[0], w_ref[0:COLS], NN)
    for index in range(1, HEAD_SIZE):
        acc += product(grads[index], w_ref[index * COLS : (index + 1) * COLS], NN)
    to_pieces([acc[:, t * LANES : (t + 1) * LANES] for t in range(3)], packs.at[DO])
    for j in range(2):
        swap_start(DO, j, packs.at[DO, j], do_in.at[y_low])
    for index in range(HEAD_SIZE):
        grads_t[index] = grads[index].astype(F32).T.astype(BF16)

    def backward_unit(i, h):
        tile, first, unit = place(i, h)
        query = q_tr[unit]
        d_out = (do_tr[unit].astype(F32) * inverse[unit]).astype(BF16)
        do_tr[unit] = d_out
        d_half = do_tr[unit, pl.ds(first, HEAD_DIM), :].astype(F32)
        att_half = att_tr[i, tile, pl.ds(first, HEAD_DIM), :].astype(BF16).astype(F32)
        delta = jnp.sum(d_half * att_half, axis=0, keepdims=True)
        acc = jnp.zeros((HEAD_DIM, SPAN), F32)
        for j in range(WINDOW):
            part = weights[unit, j]
            d_part = product(v_nat[tile, i + j], d_out, NN)
            d_score = (part.astype(F32) * (d_part - delta)).astype(BF16)
            dk_acc[tile, i + j] += product(d_score, query, NT)
            dv_acc[tile, i + j] += product(part, d_out, NT)
            acc += product(k_tr[tile, i + j, pl.ds(first, HEAD_DIM), :], d_score, NN)
        dq_tr[i, tile, pl.ds(first, HEAD_DIM), :] = acc * (HEAD_DIM**-0.5)

    for j in range(2):
        swap_wait(ATT, j, att_in.at[j])
    from_pieces(att_in, attended)
    att = attended[...]

    def projection(index):
        weight = w_ref[pl.ds(pl.multiple_of(index * COLS, COLS), COLS), :]
        return product(att, weight, NT)

    block = x_terms.shape[2]
    x_cols = x_terms.shape[3]
    per_z = X_SIZE * block
    for index in range(HEAD_SIZE):
        term = product(grads_t[index], att, NN).astype(BF16)
        for part in range(COLS // per_z):
            for x in range(X_SIZE):
                start = part * per_z + x * block
                z = index * (COLS // per_z) + part
                x_terms[z, x] = term[start : start + block, :x_cols]
                z_terms[z, x] = term[start : start + block, x_cols:]
    x_copies = []
    for step in range(1, X_SIZE):
        x_copies.append(
            send(
                x_terms.at[:, x_peer(step)],
                x_in.at[step - 1],
                x_sems.at[0, step - 1],
                x_sems.at[1, step - 1],
                device(z_at, x_peer(step), y_at),
            )
        )
    z_first_copies = []
    for step in range(1, z_size):
        z_first_copies.append(
            send(
                z_terms.at[z_peer(step)],
                z_first_in.at[step - 1],
                z_first_sems.at[0, step - 1],
                z_first_sems.at[1, step - 1],
                device(z_peer(step), x_at, y_at),
            )
        )
    for at, index in enumerate((2 * (1 - high) + 1 - core, 2 * high + 1 - core)):
        proj_send[at] = projection(index).astype(BF16)
        send(proj_send.at[at], proj_in.at[at], proj_send_sems.at[at], proj_recv_sems.at[at], sibling)
    proj_keep[0] = projection(own_across)
    proj_keep[1] = projection(own)

    for j in range(2):
        swap_wait(DO, j, do_in.at[j])
        turn(do_in, do_tr, j)
    for i in range(2):
        pl.loop(0, 3)(functools.partial(backward_unit, i))
        pack_turned(dq_tr, DQ, i)
        swap_start(DQ, i, packs.at[DQ, i], dq_in.at[y_low])
        if i == 0:
            remote(proj_send.at[0], proj_in.at[0], proj_send_sems.at[0], proj_recv_sems.at[0], sibling).wait_recv()
            hip_send[...] = (proj_keep[0] + proj_in[0].astype(F32)).astype(BF16)
            hip_copy = send(hip_send, hip_in, proj_send_sems.at[2], proj_recv_sems.at[2], across)

    accs = (dk_acc, dv_acc)

    def term_copy(at, j):
        return remote(
            near_send.at[at, j], near_in.at[at, j], term_sems.at[0, at, j], term_sems.at[1, at, j], sibling
        )

    def back_copy(at, j, target):
        return remote(
            back_send.at[at, j], back_in.at[at, j], back_sems.at[0, at, j], back_sems.at[1, at, j], target
        )

    def send_back(summed):
        for at in range(2):
            for j in range(2):
                tile = accs[at][0, j]
                third = fold(accs[at][1, j])
                if summed:
                    term_copy(at, j).wait_recv()
                    tile += near_in[at, j, :SPAN].astype(F32)
                    third += near_in[at, j, SPAN:].astype(F32)
                back_send[at, j, :SPAN] = tile.astype(BF16)
                back_send[at, j, SPAN:] = third.astype(BF16)
                pl.when(has_before)(back_copy(at, j, before).start)

    for at in range(2):
        for j in range(2):
            near_send[at, j, :SPAN] = accs[at][0, 2 + j].astype(BF16)
            near_send[at, j, SPAN:] = fold(accs[at][1, 2 + j]).astype(BF16)
            copy = term_copy(at, j)
            copy.start()
            started.append(copy)
            waits.append((has_before, back_copy(at, j, before).wait_send))
    pl.when(core == 0)(functools.partial(send_back, False))
    pl.when(core == 1)(functools.partial(send_back, True))

    for copy in x_copies:
        copy.wait_recv()
    for z in range(z_size):
        total = x_terms[z, x_at].astype(F32)
        for step in range(1, X_SIZE):
            total += x_in[step - 1, z].astype(F32)
        z_send[z] = total.astype(BF16)
    z_copies = []
    for step in range(1, z_size):
        z_copies.append(
            send(
                z_send.at[z_peer(step)],
                z_in.at[step - 1],
                z_sems.at[0, step - 1],
                z_sems.at[1, step - 1],
                device(z_peer(step), x_at, y_at),
            )
        )
    for copy in z_first_copies:
        copy.wait_recv()
    for x in range(X_SIZE):
        total = z_terms[z_at, x].astype(F32)
        for step in range(1, z_size):
            total += z_first_in[step - 1, x].astype(F32)
        x_send[x] = total.astype(BF16)
    x_last_copies = []
    for step in range(1, X_SIZE):
        x_last_copies.append(
            send(
                x_send.at[x_peer(step)],
                x_last_in.at[step - 1],
                x_last_sems.at[0, step - 1],
                x_last_sems.at[1, step - 1],
                device(z_at, x_peer(step), y_at),
            )
        )

    def finish(near):
        for at in range(2):
            for j in range(2):
                tile = accs[at][0, 4 + j]
                third = fold(accs[at][1, 4 + j])
                if near:
                    term_copy(at, j).wait_recv()
                    tile += near_in[at, j, :SPAN].astype(F32)
                    third += near_in[at, j, SPAN:].astype(F32)
                pl.when(has_after)(back_copy(at, j, after).wait_recv)
                tile += back_in[at, j, :SPAN].astype(F32)
                third += back_in[at, j, SPAN:].astype(F32)
                kind = (DK, DV)[at]
                packs[kind, j, :SPAN] = tile.astype(BF16)
                packs[kind, j, SPAN:] = third.astype(BF16)
                swap_start(kind, j, packs.at[kind, j], (dk_in, dv_in)[at].at[y_low])

    finish_waits = len(waits)
    pl.when(core == 0)(functools.partial(finish, True))
    del waits[finish_waits:]
    pl.when(core == 1)(functools.partial(finish, False))
    del waits[finish_waits:]
    for kind, buffer in ((DK, dk_in), (DV, dv_in)):
        for j in range(2):
            src = packs.at[kind, j]
            copy = remote(src, src, a2a_send_sems.at[kind, j], a2a_recv_sems.at[kind, y_low], partners[j])
            waits.append((jnp.logical_not(is_self[j]), copy.wait_send))

    for copy in z_copies:
        copy.wait_recv()
    sums[:, :x_cols] = z_send[z_at].astype(F32)
    for step in range(1, z_size):
        sums[:, :x_cols] += z_in[step - 1].astype(F32)
    for copy in x_last_copies:
        copy.wait_recv()
    sums[:, x_cols:] = x_send[x_at].astype(F32)
    for step in range(1, X_SIZE):
        sums[:, x_cols:] += x_last_in[step - 1].astype(F32)
    out_rows = dw_ref.shape[0]
    for piece in range(Y_SIZE):
        y_send[piece, 0:out_rows] = sums[piece * out_rows : (piece + 1) * out_rows]
    y_copies = []
    for step in range(1, Y_SIZE):
        y_copies.append(
            send(
                y_send.at[y_peer(step)],
                y_in.at[step - 1],
                y_sems.at[0, step - 1],
                y_sems.at[1, step - 1],
                device(z_at, x_at, y_peer(step)),
            )
        )

    for j in range(2):
        swap_wait(DQ, j, dq_in.at[j])
    from_pieces(dq_in, dq_ref)
    remote(proj_send.at[1], proj_in.at[1], proj_send_sems.at[1], proj_recv_sems.at[1], sibling).wait_recv()
    hip_copy.wait_recv()
    proj_ref[...] = (proj_keep[1] + proj_in[1].astype(F32) + hip_in[...].astype(F32)).astype(BF16)
    for j in range(2):
        swap_wait(DK, j, dk_in.at[j])
    from_pieces(dk_in, dk_ref)
    for j in range(2):
        swap_wait(DV, j, dv_in.at[j])
    from_pieces(dv_in, dv_ref)
    result = y_send[y_at]
    for step in range(1, Y_SIZE):
        y_copies[step - 1].wait_recv()
        result += y_in[step - 1]
    dw_ref[...] = result[0:out_rows]

    for copy in started:
        copy.wait_send()
    for sent, wait in waits:
        pl.when(sent)(wait)


def results_kernel(*refs):
    sems = refs[-1]
    count = (len(refs) - 1) // 2
    copies = [pltpu.make_async_copy(refs[at], refs[count + at], sems.at[at]) for at in range(count)]
    for copy in copies:
        copy.start()
    for copy in copies:
        copy.wait()


def shards(query_rows, key_rows, value_rows, out_weight, out_grad):
    seq_size = lax.axis_size("seq")
    z_size = seq_size // (X_SIZE * Y_SIZE)
    out_rows = out_weight.shape[0] // seq_size
    block = out_rows * Y_SIZE
    padded = (out_rows + 7) // 8 * 8
    x_cols = 2 * LANES
    rows_out = jax.ShapeDtypeStruct((SPAN, COLS), BF16)
    vmem = pltpu.VMEM
    dma = pltpu.SemaphoreType.DMA
    piece = (PIECE, LANES)
    scratch = [
        vmem((SPAN, COLS), BF16),
        vmem((SPAN, COLS), BF16),
        vmem((SPAN, COLS), BF16),
        vmem(out_weight.shape, BF16),
        vmem((8, 2) + piece, BF16),
        vmem((2,) + piece, BF16),
        vmem((2,) + piece, BF16),
        vmem((SLOTS,) + piece, BF16),
        vmem((SLOTS,) + piece, BF16),
        vmem((2,) + piece, BF16),
        vmem((2,) + piece, BF16),
        vmem((2,) + piece, BF16),
        vmem((2,) + piece, BF16),
        vmem((HEAD_SIZE, SPAN, COLS), BF16),
        vmem((HEAD_SIZE, COLS, SPAN), BF16),
        vmem((2, SLOTS, SPAN, LANES), BF16),
        vmem((2, SLOTS, SPAN, LANES), BF16),
        vmem((2, SLOTS, LANES, SPAN), BF16),
        vmem((2, SLOTS, LANES, SPAN), BF16),
        vmem((6, LANES, SPAN), BF16),
        vmem((6, LANES, SPAN), BF16),
        vmem((WINDOW, SPAN, SPAN), F32),
        vmem((6, WINDOW, SPAN, SPAN), BF16),
        vmem((6, 1, SPAN), F32),
        vmem((2, 2, LANES, SPAN), F32),
        vmem((2, 2, LANES, SPAN), F32),
        vmem((2, SLOTS, SPAN, LANES), F32),
        vmem((2, SLOTS, SPAN, LANES), F32),
        vmem((2, 2) + piece, BF16),
        vmem((2, 2) + piece, BF16),
        vmem((2, 2) + piece, BF16),
        vmem((2, 2) + piece, BF16),
        vmem((SPAN, COLS), BF16),
        vmem((2, SPAN, COLS), BF16),
        vmem((2, SPAN, COLS), BF16),
        vmem((2, SPAN, COLS), F32),
        vmem((SPAN, COLS), BF16),
        vmem((SPAN, COLS), BF16),
        vmem((z_size, X_SIZE, block, x_cols), BF16),
        vmem((X_SIZE - 1, z_size, block, x_cols), BF16),
        vmem((z_size, block, x_cols), BF16),
        vmem((z_size - 1, block, x_cols), BF16),
        vmem((z_size, X_SIZE, block, COLS - x_cols), BF16),
        vmem((z_size - 1, X_SIZE, block, COLS - x_cols), BF16),
        vmem((X_SIZE, block, COLS - x_cols), BF16),
        vmem((X_SIZE - 1, block, COLS - x_cols), BF16),
        vmem((Y_SIZE, padded, COLS), F32),
        vmem((Y_SIZE - 1, padded, COLS), F32),
        vmem((block, COLS), F32),
        dma((5,)),
        dma((8, 2)),
        dma((8, 2)),
        dma((2, 2, 2)),
        dma((2, 2, 2)),
        dma((2, 2, 2)),
        dma((2, 2, 2)),
        dma((3,)),
        dma((3,)),
        dma((3,)),
        dma((3,)),
        dma((2, X_SIZE - 1)),
        dma((2, z_size - 1)),
        dma((2, z_size - 1)),
        dma((2, X_SIZE - 1)),
        dma((2, Y_SIZE - 1)),
    ]
    outputs = (rows_out,) * 4 + (jax.ShapeDtypeStruct((out_rows, COLS), F32),)
    anywhere = pl.BlockSpec(memory_space=pl.ANY)
    results = pl.pallas_call(
        functools.partial(layer_kernel, z_size),
        out_shape=outputs,
        in_specs=[anywhere] * 5,
        out_specs=(pl.BlockSpec(memory_space=pltpu.VMEM),) * 5,
        scratch_shapes=scratch,
        compiler_params=pltpu.CompilerParams(
            collective_id=0, has_side_effects=True, vmem_limit_bytes=53 * 1024 * 1024
        ),
    )(query_rows, key_rows, value_rows, out_weight, out_grad)
    return pl.pallas_call(
        results_kernel,
        out_shape=outputs,
        in_specs=[pl.BlockSpec(memory_space=pltpu.VMEM)] * 5,
        out_specs=(anywhere,) * 5,
        scratch_shapes=[dma((5,))],
        compiler_params=pltpu.CompilerParams(vmem_limit_bytes=4 * 1024 * 1024),
    )(*results)


def solution(mesh):
    in_specs = (
        P("seq", "head"),
        P("seq", "head"),
        P("seq", "head"),
        P(None, "head"),
        P("seq", "head"),
    )
    out_specs = (
        P("seq", "head"),
        P("seq", "head"),
        P("seq", "head"),
        P("seq", "head"),
        P("seq", "head"),
    )
    return jax.shard_map(shards, mesh=mesh, in_specs=in_specs, out_specs=out_specs, check_vma=False)
```
